32 devices in a mesh: blk: 8 (over y, x, core), grp: 4 (over z).
Axes of the slice: x: 2, y: 2, z: 4, core: 2. Of those that a mesh axis runs over, the one named last changes fastest.
Arguments:
- user_factors: float32 [32768, 128], P(('blk', 'grp')), may hold values from -1.8 to 1.8
- user_accum: float32 [32768], P(('blk', 'grp')), may hold values from 10 to 200
- friend_factors: float32 [32768, 128], P(('blk', 'grp')), may hold values from -1.8 to 1.8
- friend_accum: float32 [32768], P(('blk', 'grp')), may hold values from 10 to 200
- item_factors: float32 [4096, 128], P('blk'), may hold values from -1.8 to 1.8
- item_accum: float32 [4096], P('blk'), may hold values from 10 to 200
- rating_values: bfloat16 [2, 1024, 128, 128], P(None, ('blk', 'grp')), may hold values from -4 to 4
- rating_masks: int32 [2, 1024, 10, 128], P(None, ('blk', 'grp')), may hold values from 0 to 16383, as said below
- rating_rows: int32 [2, 1024], P(None, ('blk', 'grp')), may hold values from 0 to 7, as said below
- rating_cols: int32 [2, 1024], P(None, ('blk', 'grp')), may hold values from 0 to 3, as said below
- rating_counts: int32 [2, 32], P(None, ('blk', 'grp')), may hold values from 1 to 32, as said below
- trust_values: bfloat16 [1536, 128, 128], P(('blk', 'grp')), may hold values from 0 to 1
- trust_masks: int32 [1536, 10, 128], P(('blk', 'grp')), may hold values from 0 to 16383, as said below
- trust_rows: int32 [1536], P(('blk', 'grp')), may hold values from 0 to 7, as said below
- trust_cols: int32 [1536], P(('blk', 'grp')), may hold values from 0 to 7, as said below
- trust_counts: int32 [32], P(('blk', 'grp')), may hold values from 1 to 48, as said below
Outputs:
- user_out: float32 [32768, 128], P(('blk', 'grp'))
- user_acc_out: float32 [32768], P(('blk', 'grp'))
- friend_out: float32 [32768, 128], P(('blk', 'grp'))
- friend_acc_out: float32 [32768], P(('blk', 'grp'))
- item_out: float32 [4096, 128], P(('blk', 'grp'))
- item_acc_out: float32 [4096], P(('blk', 'grp'))
The draws below stay inside these ranges and needn't reach their ends.
Inputs may be any that keep to these rules, and one draw needn't show every extreme that they name: `rating_rows`: in each stratum and group the listed (row, column) tile pairs of all slots are distinct. `rating_cols`: see rating_rows. `rating_counts`: slots at or past the count are ignored; in each stratum some group has all 32 slots live. `rating_masks`: bit i of word w at column c marks row 14 w + i of the tile; bits of rows at or past 128 are zero. `trust_rows`: in each group the listed (row, column) tile pairs of all slots are distinct. `trust_cols`: see trust_rows. `trust_counts`: slots at or past the count are ignored; some group has all 48 slots live. `trust_masks`: bit i of word w at column c marks row 14 w + i of the tile; bits of rows at or past 128 are zero.
All inputs are finite; a program needn't handle non-finite values.
Results may differ from the reference program's by a relative error of at most 0.005.
Values may be sent and summed in bfloat16 or wider, within the bound.
A program may use at most 64 MiB of HBM per device.

```python
import math
import jax
import jax.numpy as jnp
from jax import lax

FACTOR_RANK = 128
TILE_SIZE = 128
USER_ROWS = 1024
ITEM_ROWS = 512
RATE_SLOTS = 32
SOCIAL_SLOTS = 48
MASK_WORDS = 10
ALL_USERS = 32768
ALL_ITEMS = 4096
N_BLK = 8
N_GRP = 4
DEVICES = 32


def tile_places(key, lanes, slot_total, height, across):
    lane_keys = jax.random.split(key, lanes)

    def choose(lane_key):
        return jax.random.permutation(lane_key, height * across)[:slot_total]
    return jax.vmap(choose)(lane_keys).reshape(-1)


def rating_places(key):
    places = tile_places(jax.random.fold_in(key, 17), 2 * DEVICES, RATE_SLOTS, USER_ROWS // TILE_SIZE, ITEM_ROWS // TILE_SIZE)
    return places.reshape(2, RATE_SLOTS * DEVICES)


def trust_places(key):
    return tile_places(jax.random.fold_in(key, 23), DEVICES, SOCIAL_SLOTS, USER_ROWS // TILE_SIZE, USER_ROWS // TILE_SIZE)


def skewed_counts(key, lines, slot_total):
    key_one, key_two, key_three = jax.random.split(key, 3)
    density = jax.random.randint(key_one, (lines, DEVICES), 0, 4)
    base_count = jnp.maximum(slot_total // jnp.left_shift(1, density), 1)
    jitter = jax.random.randint(key_two, (lines, DEVICES), 0, base_count // 4 + 1)
    counts = jnp.maximum(base_count - jitter, 1)
    chosen = jax.random.randint(key_three, (lines, 1), 0, DEVICES)
    positions = jnp.arange(DEVICES)[None, :]
    return jnp.where(positions == chosen, slot_total, counts).astype(jnp.int32)


def packed_bits(key, leading):
    key_one, key_two, key_three = jax.random.split(key, 3)
    full_shape = leading + (MASK_WORDS, TILE_SIZE)
    top_bits = jax.random.randint(key_one, full_shape, 0, 16384)
    low_bits = jax.random.randint(key_two, full_shape, 0, 16384)
    density = jax.random.randint(key_three, leading + (1, 1), 0, 3)
    packed_words = jnp.where(density == 0, top_bits & low_bits, jnp.where(density == 1, top_bits, top_bits | low_bits))
    kept_rows = TILE_SIZE - 14 * (MASK_WORDS - 1)
    word_limit = jnp.where(jnp.arange(MASK_WORDS) == MASK_WORDS - 1, 2 ** kept_rows - 1, 16383)
    return (packed_words & word_limit[:, None]).astype(jnp.int32)


def draw_rating_rows(key, part):
    return (rating_places(key) // (ITEM_ROWS // TILE_SIZE)).astype(jnp.int32)


def draw_rating_cols(key, part):
    return (rating_places(key) % (ITEM_ROWS // TILE_SIZE)).astype(jnp.int32)


def draw_rating_counts(key, part):
    return skewed_counts(jax.random.fold_in(key, 29), 2, RATE_SLOTS)


def draw_rating_masks(key, part):
    return packed_bits(jax.random.fold_in(key, 41), (2, RATE_SLOTS * DEVICES))


def draw_trust_rows(key, part):
    return (trust_places(key) // (USER_ROWS // TILE_SIZE)).astype(jnp.int32)


def draw_trust_cols(key, part):
    return (trust_places(key) % (USER_ROWS // TILE_SIZE)).astype(jnp.int32)


def draw_trust_counts(key, part):
    return skewed_counts(jax.random.fold_in(key, 31), 1, SOCIAL_SLOTS).reshape(DEVICES)


def draw_trust_masks(key, part):
    return packed_bits(jax.random.fold_in(key, 43), (SOCIAL_SLOTS * DEVICES,))


def block_levels(stream_key, dims, pieces, smallest, high):
    gain = 1.0
    for dim, parts in pieces:
        steps = jax.random.uniform(jax.random.fold_in(jax.random.fold_in(stream_key, 6), dim), (parts,), jnp.float32, smallest / len(pieces), high / len(pieces))
        gain = gain * jnp.repeat(jnp.exp(steps), dims[dim] // parts).reshape((-1,) + (1,) * (len(dims) - 1 - dim))
    return gain


def gaussian(rng, dims, spread, most, shards=(), kind=jnp.bfloat16):
    gain = block_levels(rng, dims, shards, -0.22, 0.18) if shards else 1.0
    values = jax.random.normal(rng, dims, jnp.float32) * spread * gain
    return jnp.minimum(jnp.maximum(values, -most), most).astype(kind)


def setup_inputs(seed: int = 0) -> dict:
    streams_of = jax.random.split(jax.random.key(seed), 17)
    user_factors = gaussian(streams_of[0], (ALL_USERS, FACTOR_RANK), 0.3, 1.8, ((0, 32),), jnp.float32)
    user_accum = jnp.clip(jnp.exp(math.log(200.0) - 2.9957323 * jax.random.uniform(streams_of[1], (ALL_USERS,), jnp.float32) ** block_levels(streams_of[1], (ALL_USERS,), ((0, 32),), -0.2, 0.2)), 10.0, 200.0)
    friend_factors = gaussian(streams_of[2], (ALL_USERS, FACTOR_RANK), 0.3, 1.8, ((0, 32),), jnp.float32)
    friend_accum = jnp.clip(jnp.exp(math.log(200.0) - 2.9957323 * jax.random.uniform(streams_of[3], (ALL_USERS,), jnp.float32) ** block_levels(streams_of[3], (ALL_USERS,), ((0, 32),), -0.2, 0.2)), 10.0, 200.0)
    item_factors = gaussian(streams_of[4], (ALL_ITEMS, FACTOR_RANK), 0.3, 1.8, ((0, 8),), jnp.float32)
    item_accum = jnp.clip(jnp.exp(math.log(200.0) - 2.9957323 * jax.random.uniform(streams_of[5], (ALL_ITEMS,), jnp.float32) ** block_levels(streams_of[5], (ALL_ITEMS,), ((0, 8),), -0.2, 0.2)), 10.0, 200.0)
    rating_values = gaussian(streams_of[6], (2, RATE_SLOTS * DEVICES, TILE_SIZE, TILE_SIZE), 1.0, 4.0, ((1, 32),))
    rating_masks = draw_rating_masks(jax.random.fold_in(streams_of[16], 71), 0)
    rating_rows = draw_rating_rows(jax.random.fold_in(streams_of[16], 71), 0)
    rating_cols = draw_rating_cols(jax.random.fold_in(streams_of[16], 71), 0)
    rating_counts = draw_rating_counts(jax.random.fold_in(streams_of[16], 71), 0)
    trust_values = jnp.clip(1.0 * jax.random.uniform(streams_of[11], (SOCIAL_SLOTS * DEVICES, TILE_SIZE, TILE_SIZE), jnp.float32) ** block_levels(streams_of[11], (SOCIAL_SLOTS * DEVICES, TILE_SIZE, TILE_SIZE), ((0, 32),), -0.2, 0.2), 0.0, 1.0).astype(jnp.bfloat16)
    trust_masks = draw_trust_masks(jax.random.fold_in(streams_of[16], 71), 0)
    trust_rows = draw_trust_rows(jax.random.fold_in(streams_of[16], 71), 0)
    trust_cols = draw_trust_cols(jax.random.fold_in(streams_of[16], 71), 0)
    trust_counts = draw_trust_counts(jax.random.fold_in(streams_of[16], 71), 0)
    return {"user_factors": user_factors, "user_accum": user_accum, "friend_factors": friend_factors, "friend_accum": friend_accum, "item_factors": item_factors, "item_accum": item_accum, "rating_values": rating_values, "rating_masks": rating_masks, "rating_rows": rating_rows, "rating_cols": rating_cols, "rating_counts": rating_counts, "trust_values": trust_values, "trust_masks": trust_masks, "trust_rows": trust_rows, "trust_cols": trust_cols, "trust_counts": trust_counts}


learn_rate = 0.3
shrinkage = 0.02

def unpack_bits(packed_words):
    shifts = jnp.arange(14, dtype=jnp.int32)
    mask_bits = jnp.bitwise_and(jnp.right_shift(packed_words[..., :, None, :], shifts[:, None]), 1)
    mask_bits = mask_bits.reshape(packed_words.shape[:-2] + (packed_words.shape[-2] * 14, packed_words.shape[-1]))
    return mask_bits[..., :TILE_SIZE, :]

def tile_products(left_low, right_low, values, packed_words, tile_rows, tile_cols, live_total):
    slot_total = values.shape[0]
    left_tiles = left_low.reshape(-1, TILE_SIZE, FACTOR_RANK)
    right_tiles = right_low.reshape(-1, TILE_SIZE, FACTOR_RANK)
    left_pick = jnp.take(left_tiles, tile_rows, axis=0).astype(jnp.float32)
    right_pick = jnp.take(right_tiles, tile_cols, axis=0).astype(jnp.float32)
    predict = jnp.einsum('sik,sjk->sij', left_pick, right_pick, precision=lax.Precision.HIGHEST)
    live_slots = (jnp.arange(slot_total, dtype=jnp.int32) < live_total).astype(jnp.float32)
    observed = unpack_bits(packed_words).astype(jnp.float32) * live_slots[:, None, None]
    residual = (observed * (values.astype(jnp.float32) - predict)).astype(jnp.bfloat16)
    residual = lax.optimization_barrier(residual).astype(jnp.float32)
    left_part = jnp.einsum('sij,sjk->sik', residual, right_pick, precision=lax.Precision.HIGHEST)
    right_part = jnp.einsum('sij,sik->sjk', residual, left_pick, precision=lax.Precision.HIGHEST)
    left_sum = jnp.zeros(left_tiles.shape, jnp.float32).at[tile_rows].add(left_part)
    right_sum = jnp.zeros(right_tiles.shape, jnp.float32).at[tile_cols].add(right_part)
    return (left_sum.reshape(-1, FACTOR_RANK), right_sum.reshape(-1, FACTOR_RANK))

def row_update(factor, accum, gradient):
    new_accum = accum + lax.optimization_barrier(jnp.mean(gradient * gradient, axis=-1))
    return (factor - learn_rate * gradient / jnp.sqrt(new_accum)[..., None], new_accum)

def per_device(array):
    return array.reshape((N_BLK, N_GRP, -1) + array.shape[1:])

def rating_stratum(user_state, user_acc, item_state, item_acc, values, packed_words, tile_rows, tile_cols, live_counts, offset):
    user_split = user_state.astype(jnp.bfloat16).reshape(N_BLK, N_GRP, USER_ROWS, FACTOR_RANK)
    item_blocks = jnp.roll(item_state.astype(jnp.bfloat16).reshape(N_BLK, ITEM_ROWS, FACTOR_RANK), offset, axis=0)

    def one_block(packed):
        user_block, item_block, value_block, word_block, row_block, col_block, count_block = packed

        def one_group(user_group, value_group, word_group, row_group, col_group, count_group):
            return tile_products(user_group, item_block, value_group, word_group, row_group, col_group, count_group)
        user_part, item_part = jax.vmap(one_group)(user_block, value_block, word_block, row_block, col_block, count_block)
        return (user_part, lax.optimization_barrier(jnp.sum(item_part, axis=0)))
    user_prod, item_prod = lax.map(one_block, (user_split, item_blocks, per_device(values), per_device(packed_words), per_device(tile_rows), per_device(tile_cols), live_counts.reshape(N_BLK, N_GRP)))
    item_prod = jnp.roll(item_prod, -offset, axis=0).reshape(ALL_ITEMS, FACTOR_RANK)
    user_prod = user_prod.reshape(ALL_USERS, FACTOR_RANK)
    user_state, user_acc = row_update(user_state, user_acc, shrinkage * user_state - user_prod)
    item_state, item_acc = row_update(item_state, item_acc, shrinkage * item_state - item_prod)
    return (user_state, user_acc, item_state, item_acc)

def reference(user_factors, user_accum, friend_factors, friend_accum, item_factors, item_accum, rating_values, rating_masks, rating_rows, rating_cols, rating_counts, trust_values, trust_masks, trust_rows, trust_cols, trust_counts):
    user_state, user_acc, item_state, item_acc = (user_factors, user_accum, item_factors, item_accum)
    for stratum in range(2):
        user_state, user_acc, item_state, item_acc = rating_stratum(user_state, user_acc, item_state, item_acc, rating_values[stratum], rating_masks[stratum], rating_rows[stratum], rating_cols[stratum], rating_counts[stratum], stratum)
    user_split = user_state.astype(jnp.bfloat16).reshape(N_BLK, N_GRP, USER_ROWS, FACTOR_RANK)
    partner = jnp.bitwise_xor(jnp.arange(N_BLK, dtype=jnp.int32), N_BLK // 2)
    friend_split = friend_factors.astype(jnp.bfloat16).reshape(N_BLK, N_GRP, USER_ROWS, FACTOR_RANK)[partner]

    def one_block(packed):
        user_block, friend_block, value_block, word_block, row_block, col_block, count_block = packed
        return jax.vmap(tile_products)(user_block, friend_block, value_block, word_block, row_block, col_block, count_block)
    user_prod, friend_prod = lax.map(one_block, (user_split, friend_split, per_device(trust_values), per_device(trust_masks), per_device(trust_rows), per_device(trust_cols), trust_counts.reshape(N_BLK, N_GRP)))
    friend_prod = friend_prod[partner].reshape(ALL_USERS, FACTOR_RANK)
    user_prod = user_prod.reshape(ALL_USERS, FACTOR_RANK)
    user_out, user_acc_out = row_update(user_state, user_acc, shrinkage * user_state - user_prod)
    friend_out, friend_acc_out = row_update(friend_factors, friend_accum, shrinkage * friend_factors - friend_prod)
    item_out = jnp.roll(item_state.reshape(N_BLK, ITEM_ROWS, FACTOR_RANK), 1, axis=0).reshape(ALL_ITEMS, FACTOR_RANK)
    item_acc_out = jnp.roll(item_acc.reshape(N_BLK, ITEM_ROWS), 1, axis=0).reshape(ALL_ITEMS)
    return (user_out, user_acc_out, friend_out, friend_acc_out, item_out, item_acc_out)
```

```python
import functools

import jax
import jax.numpy as jnp
from jax import lax
from jax.experimental import pallas as pl
from jax.experimental.pallas import tpu as pltpu
from jax.sharding import PartitionSpec as P

learn_rate = 0.3
shrinkage = 0.02
word_bits = 14
MESH = pl.DeviceIdType.MESH
f32, bf16 = jnp.float32, jnp.bfloat16


def slot_table(tile_rows, tile_cols, live_total, row_tiles, col_tiles):
    slots = jnp.arange(tile_rows.shape[0], dtype=jnp.int32)
    places = jnp.arange(row_tiles * col_tiles, dtype=jnp.int32)
    hit = (tile_rows * col_tiles + tile_cols)[None, :] == places[:, None]
    hit = hit & (slots < live_total)[None, :]
    return jnp.sum(jnp.where(hit, slots + 1, 0), axis=1, dtype=jnp.int32)


def spread(words, edge):
    sub = lax.broadcasted_iota(jnp.int32, (8, words.shape[1]), 0)
    pieces = []
    for first in range(0, edge, 8):
        low, high = first // word_bits, (first + 7) // word_bits
        piece = jnp.broadcast_to(words[low : low + 1], sub.shape)
        if high != low:
            after = jnp.broadcast_to(words[high : high + 1], sub.shape)
            piece = jnp.where(sub < high * word_bits - first, piece, after)
        pieces.append(piece)
    return jnp.concatenate(pieces, axis=0)


def as_columns(row, edge):
    return jnp.broadcast_to(row, (edge, edge)).T


def row_update(factor, accum, gradient):
    new_accum = accum + jnp.mean(gradient * gradient, axis=-1, keepdims=True)
    return factor - learn_rate * gradient * lax.rsqrt(new_accum), new_accum


def strata_kernel(
    blocks, groups,
    table, user_accum, friend_accum, item_accum,
    user_hbm, friend_hbm, item_hbm, rate_values, rate_masks, trust_values, trust_masks,
    user_out, user_acc_out, friend_out, friend_acc_out, item_out, item_acc_out,
    user, user_acc, user_low, user_t, friend, friend_low, far_low, item, item_low, item_next,
    values_0, values_1, values_2, masks_0, masks_1, masks_2, bits, residual,
    part, gathered, share_low, ship, shipped, far_part, friend_part,
    load_sem, far_send, far_recv, part_send, part_recv, low_send, low_recv,
    ship_send, ship_recv, back_send, back_recv,
):
    b, g = lax.axis_index("blk"), lax.axis_index("grp")
    after = lax.rem(b + 1, blocks)
    before = lax.rem(b + blocks - 1, blocks)
    partner = lax.rem(b + blocks // 2, blocks)
    edge = bits.shape[0]
    wide = 2 * edge
    user_rows, item_rows, friend_rows = user.shape[0], item.shape[0], friend.shape[0]
    user_tiles, item_tiles = user_rows // edge, item_rows // edge
    friend_tiles = friend_rows // edge

    barrier = pltpu.get_barrier_semaphore()
    for step in range(1, groups):
        pl.semaphore_signal(
            barrier, inc=1, device_id=(b, lax.rem(g + step, groups)), device_id_type=MESH
        )
    for other in range(groups):
        pl.semaphore_signal(barrier, inc=1, device_id=(before, other), device_id_type=MESH)
    pl.semaphore_signal(barrier, inc=1, device_id=(partner, g), device_id_type=MESH)

    pairs = [
        (friend_hbm, friend), (user_hbm, user), (item_hbm, item),
        (rate_masks.at[0], masks_0), (rate_values.at[0], values_0),
        (rate_masks.at[1], masks_1), (rate_values.at[1], values_1),
        (trust_masks, masks_2), (trust_values, values_2),
    ]
    loads = [
        pltpu.make_async_copy(src, dst, load_sem.at[n]) for n, (src, dst) in enumerate(pairs)
    ]
    for load in loads:
        load.start()

    place = lax.broadcasted_iota(jnp.int32, bits.shape, 0)
    bits[...] = jnp.left_shift(jnp.ones_like(place), lax.rem(place, word_bits))

    loads[0].wait()
    friend_low[...] = friend[...].astype(bf16)
    pl.semaphore_wait(barrier, 2 * groups)
    far_copy = pltpu.make_async_remote_copy(
        src_ref=friend_low, dst_ref=far_low, send_sem=far_send, recv_sem=far_recv,
        device_id=(partner, g), device_id_type=MESH,
    )
    far_copy.start()

    def keep_user(rows, state):
        low = state.astype(bf16)
        user_low[rows, :] = low
        user_t[:, rows] = state.T.astype(bf16)

    def tile_rows(tile):
        return pl.ds(pl.multiple_of(tile * edge, edge), edge)

    loads[1].wait()

    def first_user(tile, carry):
        rows = tile_rows(tile)
        keep_user(rows, user[rows, :])
        user_acc[rows, :] = as_columns(user_accum[pl.ds(tile, 1), :], edge)
        return carry

    lax.fori_loop(0, user_tiles, first_user, 0)
    loads[2].wait()
    item_low[...] = item[...].astype(bf16)

    def right_products(right_low, values, masks, base, col_tiles, chunk):
        columns = pl.ds(chunk * wide, wide)

        def block(pair, carry):
            rows = pl.ds(pl.multiple_of(pair * wide, wide), wide)
            predict = lax.dot_general(
                user_low[rows, :], right_low[columns, :], (((1,), (1,)), ((), ())),
                preferred_element_type=f32,
            )
            for i in range(2):
                for k in range(2):
                    found = table[base + (2 * pair + i) * col_tiles + 2 * chunk + k]
                    slot = jnp.maximum(found - 1, 0)
                    words = masks[slot] * jnp.minimum(found, 1)
                    seen = (spread(words, edge) & bits[...]) != 0
                    error = (
                        values[slot].astype(f32)
                        - predict[i * edge : (i + 1) * edge, k * edge : (k + 1) * edge]
                    )
                    residual[tile_rows(2 * pair + i), pl.ds(chunk * wide + k * edge, edge)] = (
                        jnp.where(seen, error, 0.0).astype(bf16)
                    )
            return carry

        lax.fori_loop(0, user_tiles // 2, block, 0)
        return jnp.dot(user_t[...], residual[:, columns], preferred_element_type=f32)

    def update_users(right_low, width, finish):
        def block(tile, carry):
            rows = tile_rows(tile)
            product = jnp.dot(
                residual[rows, pl.ds(0, width)], right_low[...], preferred_element_type=f32
            )
            state = user[rows, :]
            state, accum = row_update(state, user_acc[rows, :], shrinkage * state - product)
            finish(tile, rows, state, accum)
            return carry

        lax.fori_loop(0, user_tiles, block, 0)

    def part_copy(stratum, owner, source):
        return pltpu.make_async_remote_copy(
            src_ref=part.at[stratum, owner], dst_ref=gathered.at[stratum, source],
            send_sem=part_send.at[stratum, owner], recv_sem=part_recv.at[stratum, source],
            device_id=(b, owner), device_id_type=MESH,
        )

    def send_parts(stratum, right_low, values, masks, base):
        for chunk in range(item_tiles // 2):
            product = right_products(right_low, values, masks, base, item_tiles, chunk)
            for k in range(2):
                owner = 2 * chunk + k
                piece = product[:, k * edge : (k + 1) * edge].T.astype(bf16)
                part[stratum, owner] = piece

                @pl.when(owner != g)
                def _():
                    part_copy(stratum, owner, g).start()

                @pl.when(owner == g)
                def _():
                    gathered[stratum, g] = piece

    def part_total(stratum):
        for source in range(groups):
            @pl.when(source != g)
            def _():
                part_copy(stratum, source, source).wait_recv()

        total = gathered[stratum, 0].astype(f32)
        for source in range(1, groups):
            total = total + gathered[stratum, source].astype(f32)
        return total

    loads[3].wait()
    loads[4].wait()
    send_parts(0, item_low, values_0, masks_0, 0)

    def middle_user(tile, rows, state, accum):
        user[rows, :] = state
        user_acc[rows, :] = accum
        keep_user(rows, state)

    update_users(item_low, item_rows, middle_user)

    share = item[tile_rows(g), :]
    share, share_acc = row_update(
        share, as_columns(item_accum[pl.ds(g, 1), :], edge), shrinkage * share - part_total(0)
    )
    share_low[...] = share.astype(bf16)
    low_copies = [
        pltpu.make_async_remote_copy(
            src_ref=share_low, dst_ref=item_next.at[tile_rows(g), :],
            send_sem=low_send.at[other], recv_sem=low_recv.at[g],
            device_id=(after, other), device_id_type=MESH,
        )
        for other in range(groups)
    ]
    for copy in low_copies:
        copy.start()
    ship[pl.ds(0, edge), :] = share
    ship[pl.ds(edge, 8), :] = share_acc.T[0:8, :]
    ship_copy = pltpu.make_async_remote_copy(
        src_ref=ship, dst_ref=shipped, send_sem=ship_send, recv_sem=ship_recv,
        device_id=(after, g), device_id_type=MESH,
    )
    ship_copy.start()

    for n in range(5, 9):
        loads[n].wait()
    for source in range(groups):
        pltpu.make_async_remote_copy(
            src_ref=share_low, dst_ref=item_next.at[pl.ds(source * edge, edge), :],
            send_sem=low_send.at[source], recv_sem=low_recv.at[source],
            device_id=(after, source), device_id_type=MESH,
        ).wait_recv()
    send_parts(1, item_next, values_1, masks_1, user_tiles * item_tiles)
    update_users(item_next, item_rows, middle_user)

    far_copy.wait_recv()

    def back_copy(chunk):
        rows = pl.ds(chunk * wide, wide)
        return pltpu.make_async_remote_copy(
            src_ref=far_part.at[rows, :], dst_ref=friend_part.at[rows, :],
            send_sem=back_send.at[chunk], recv_sem=back_recv.at[chunk],
            device_id=(partner, g), device_id_type=MESH,
        )

    for chunk in range(friend_tiles // 2):
        product = right_products(
            far_low, values_2, masks_2, 2 * user_tiles * item_tiles, friend_tiles, chunk
        )
        far_part[pl.ds(chunk * wide, wide), :] = product.T.astype(bf16)
        back_copy(chunk).start()

    def last_user(tile, rows, state, accum):
        user_out[rows, :] = state
        user_acc_out[pl.ds(tile, 1), :] = accum.T[0:1, :]

    update_users(far_low, friend_rows, last_user)

    ship_copy.wait_recv()
    share = shipped[pl.ds(0, edge), :]
    share_acc = as_columns(shipped[pl.ds(edge, 1), :], edge)
    share, share_acc = row_update(share, share_acc, shrinkage * share - part_total(1))
    item_out[...] = share
    item_acc_out[...] = share_acc.T[0:1, :]

    for chunk in range(friend_tiles // 2):
        back_copy(chunk).wait_recv()
        for k in range(2):
            tile = 2 * chunk + k
            rows = pl.ds(tile * edge, edge)
            state = friend[rows, :]
            gradient = shrinkage * state - friend_part[rows, :].astype(f32)
            accum = as_columns(friend_accum[pl.ds(tile, 1), :], edge)
            state, accum = row_update(state, accum, gradient)
            friend_out[rows, :] = state
            friend_acc_out[pl.ds(tile, 1), :] = accum.T[0:1, :]

    far_copy.wait_send()
    for stratum in range(2):
        for owner in range(groups):
            @pl.when(owner != g)
            def _():
                part_copy(stratum, owner, g).wait_send()
    for copy in low_copies:
        copy.wait_send()
    ship_copy.wait_send()
    for chunk in range(friend_tiles // 2):
        back_copy(chunk).wait_send()


def local(
    user_factors, user_accum, friend_factors, friend_accum, item_factors, item_accum,
    rating_values, rating_masks, rating_rows, rating_cols, rating_counts,
    trust_values, trust_masks, trust_rows, trust_cols, trust_counts,
):
    blocks, groups = lax.axis_size("blk"), lax.axis_size("grp")
    edge, rank = rating_values.shape[-1], user_factors.shape[-1]
    users, items, friends = (
        user_factors.shape[0], item_factors.shape[0], friend_factors.shape[0]
    )
    user_tiles, item_tiles, friend_tiles = users // edge, items // edge, friends // edge
    assert edge == rank and items == groups * edge and blocks > 2
    assert user_tiles % 2 == 0 and item_tiles % 2 == 0 and friend_tiles % 2 == 0
    table = jnp.concatenate(
        [
            slot_table(
                rating_rows[s], rating_cols[s], rating_counts[s, 0], user_tiles, item_tiles
            )
            for s in range(2)
        ]
        + [slot_table(trust_rows, trust_cols, trust_counts[0], user_tiles, friend_tiles)]
    )
    vmem = pl.BlockSpec(memory_space=pltpu.VMEM)
    anywhere = pl.BlockSpec(memory_space=pl.ANY)
    dma = pltpu.SemaphoreType.DMA
    flops = 6 * rank * users * (2 * items + friends)
    user_out, user_acc, friend_out, friend_acc, item_out, item_acc = pl.pallas_call(
        functools.partial(strata_kernel, blocks, groups),
        out_shape=[
            jax.ShapeDtypeStruct((users, rank), f32),
            jax.ShapeDtypeStruct((user_tiles, edge), f32),
            jax.ShapeDtypeStruct((friends, rank), f32),
            jax.ShapeDtypeStruct((friend_tiles, edge), f32),
            jax.ShapeDtypeStruct((edge, rank), f32),
            jax.ShapeDtypeStruct((1, edge), f32),
        ],
        in_specs=[pl.BlockSpec(memory_space=pltpu.SMEM)] + [vmem] * 3 + [anywhere] * 7,
        out_specs=[vmem] * 6,
        scratch_shapes=[
            pltpu.VMEM((users, rank), f32),
            pltpu.VMEM((users, edge), f32),
            pltpu.VMEM((users, rank), bf16),
            pltpu.VMEM((rank, users), bf16),
            pltpu.VMEM((friends, rank), f32),
            pltpu.VMEM((friends, rank), bf16),
            pltpu.VMEM((friends, rank), bf16),
            pltpu.VMEM((items, rank), f32),
            pltpu.VMEM((items, rank), bf16),
            pltpu.VMEM((items, rank), bf16),
            pltpu.VMEM(rating_values.shape[1:], bf16),
            pltpu.VMEM(rating_values.shape[1:], bf16),
            pltpu.VMEM(trust_values.shape, bf16),
            pltpu.VMEM(rating_masks.shape[1:], jnp.int32),
            pltpu.VMEM(rating_masks.shape[1:], jnp.int32),
            pltpu.VMEM(trust_masks.shape, jnp.int32),
            pltpu.VMEM((edge, edge), jnp.int32),
            pltpu.VMEM((users, max(items, friends)), bf16),
            pltpu.VMEM((2, groups, edge, rank), bf16),
            pltpu.VMEM((2, groups, edge, rank), bf16),
            pltpu.VMEM((edge, rank), bf16),
            pltpu.VMEM((edge + 8, rank), f32),
            pltpu.VMEM((edge + 8, rank), f32),
            pltpu.VMEM((friends, rank), bf16),
            pltpu.VMEM((friends, rank), bf16),
            dma((9,)),
            dma, dma,
            dma((2, groups)), dma((2, groups)),
            dma((groups,)), dma((groups,)),
            dma, dma,
            dma((friend_tiles // 2,)), dma((friend_tiles // 2,)),
        ],
        compiler_params=pltpu.CompilerParams(
            collective_id=0, has_side_effects=True, vmem_limit_bytes=48 * 1024 * 1024
        ),
        cost_estimate=pl.CostEstimate(
            flops=flops, bytes_accessed=8 * 1024 * 1024, transcendentals=0
        ),
        name="strata",
    )(
        table,
        user_accum.reshape(user_tiles, edge),
        friend_accum.reshape(friend_tiles, edge),
        item_accum.reshape(item_tiles, edge),
        user_factors, friend_factors, item_factors,
        rating_values, rating_masks, trust_values, trust_masks,
    )
    return (
        user_out, user_acc.reshape(-1), friend_out, friend_acc.reshape(-1),
        item_out, item_acc.reshape(-1),
    )


def solution(mesh):
    split = P(("blk", "grp"))
    second = P(None, ("blk", "grp"))
    return jax.shard_map(
        local,
        mesh=mesh,
        in_specs=(
            split, split, split, split, P("blk"), P("blk"),
            second, second, second, second, second,
            split, split, split, split, split,
        ),
        out_specs=(split,) * 6,
        check_vma=False,
    )
```

```python
import functools

import jax
import jax.numpy as jnp
from jax import lax
from jax.experimental import pallas as pl
from jax.experimental.pallas import tpu as pltpu
from jax.sharding import PartitionSpec as P

learn_rate = 0.3
shrinkage = 0.02
word_bits = 14
MESH = pl.DeviceIdType.MESH
f32, bf16 = jnp.float32, jnp.bfloat16


def slot_table(seats, tables, edge):
    seats[...] = jnp.full_like(seats[...], -2 * edge)
    for n, (rows, cols, count, across, _) in enumerate(tables):
        place = rows * across + cols
        slot = lax.broadcasted_iota(jnp.int32, place.shape, 1)
        seats[n : n + 1, 0 : place.shape[1]] = jnp.where(slot < count, place, -2 * edge)
    lane = lax.broadcasted_iota(jnp.int32, (edge, edge), 1)
    sub = lax.broadcasted_iota(jnp.int32, (edge, edge), 0)
    line = jnp.zeros((1, edge), jnp.int32)
    base = 0
    for n, (rows, _, _, _, places) in enumerate(tables):
        hit = as_columns(seats[n : n + 1, :], edge) == lane - base
        found = jnp.sum(jnp.where(hit, sub + 1, 0), axis=0, keepdims=True)
        entry = jnp.where(found > 0, found - 1, rows.shape[1])
        inside = (lane[0:1] >= base) & (lane[0:1] < base + places)
        line = jnp.where(inside, entry, line)
        base += places
    assert base <= edge
    return line


def spread(words, edge):
    sub = lax.broadcasted_iota(jnp.int32, (8, words.shape[2]), 0)
    pieces = []
    for first in range(0, edge, 8):
        low, high = first // word_bits, (first + 7) // word_bits
        piece = jnp.broadcast_to(words[low], sub.shape)
        if high != low:
            after = jnp.broadcast_to(words[high], sub.shape)
            piece = jnp.where(sub < high * word_bits - first, piece, after)
        pieces.append(piece)
    return jnp.concatenate(pieces, axis=0)


def as_columns(row, edge):
    return jnp.broadcast_to(row, (edge, edge)).T


def row_update(factor, accum, gradient):
    new_accum = accum + jnp.mean(gradient * gradient, axis=-1, keepdims=True)
    return factor - learn_rate * gradient * lax.rsqrt(new_accum), new_accum


def strata_kernel(
    blocks, groups,
    user_hbm, friend_hbm, item_hbm, user_accum_hbm, friend_accum_hbm, item_accum_hbm,
    rate_rows_hbm, rate_cols_hbm, rate_counts_hbm,
    trust_rows_hbm, trust_cols_hbm, trust_counts_hbm,
    rate_values, rate_masks, trust_values, trust_masks,
    user_out, user_acc_out, friend_out, friend_acc_out, item_out, item_acc_out,
    user, user_acc, user_low, user_t, friend, friend_low, far_low, item, item_low, item_next,
    values_0, values_1, values_2, masks_0, masks_1, masks_2, bits, residual,
    user_accum, friend_accum, item_accum,
    rate_rows, rate_cols, rate_counts, trust_rows, trust_cols, trust_counts,
    seats, line, table, part_0, part_1, gathered_0, gathered_1, share_low, ship, shipped, far_part, friend_part,
    load_sem, table_sem, far_send, far_recv, part_send, part_recv, low_send, low_recv,
    ship_send, ship_recv, back_send, back_recv,
):
    b, g = lax.axis_index("blk"), lax.axis_index("grp")
    after = lax.rem(b + 1, blocks)
    before = lax.rem(b + blocks - 1, blocks)
    partner = lax.rem(b + blocks // 2, blocks)
    edge = bits.shape[0]
    wide = 2 * edge
    user_rows, item_rows, friend_rows = user.shape[0], item.shape[0], friend.shape[0]
    user_tiles, item_tiles = user_rows // edge, item_rows // edge
    friend_tiles = friend_rows // edge

    barrier = pltpu.get_barrier_semaphore()
    for step in range(1, groups):
        pl.semaphore_signal(
            barrier, inc=1, device_id=(b, lax.rem(g + step, groups)), device_id_type=MESH
        )
    for other in range(groups):
        pl.semaphore_signal(barrier, inc=1, device_id=(before, other), device_id_type=MESH)
    pl.semaphore_signal(barrier, inc=1, device_id=(partner, g), device_id_type=MESH)

    part, gathered = (part_0, part_1), (gathered_0, gathered_1)
    rate_slots, trust_slots = values_0.shape[0], values_2.shape[0]
    pairs = [
        (friend_hbm, friend),
        (rate_rows_hbm, rate_rows), (rate_cols_hbm, rate_cols), (rate_counts_hbm, rate_counts),
        (trust_rows_hbm, trust_rows), (trust_cols_hbm, trust_cols),
        (trust_counts_hbm, trust_counts),
        (user_accum_hbm, user_accum), (friend_accum_hbm, friend_accum),
        (item_accum_hbm, item_accum),
        (user_hbm, user), (item_hbm, item),
        (rate_masks.at[0], masks_0.at[:, pl.ds(0, rate_slots), :]),
        (rate_values.at[0], values_0),
        (rate_masks.at[1], masks_1.at[:, pl.ds(0, rate_slots), :]),
        (rate_values.at[1], values_1),
        (trust_masks, masks_2.at[:, pl.ds(0, trust_slots), :]),
        (trust_values, values_2),
    ]
    loads = [
        pltpu.make_async_copy(src, dst, load_sem.at[n]) for n, (src, dst) in enumerate(pairs)
    ]
    for load in loads:
        load.start()

    place = lax.broadcasted_iota(jnp.int32, bits.shape, 0)
    bits[...] = jnp.left_shift(jnp.ones_like(place), lax.rem(place, word_bits))

    for masks in (masks_0, masks_1, masks_2):
        spare = masks.shape[1] - 8
        masks[:, pl.ds(spare, 8), :] = jnp.zeros((masks.shape[0], 8, edge), jnp.int32)

    loads[0].wait()
    friend_low[...] = friend[...].astype(bf16)
    pl.semaphore_wait(barrier, 2 * groups)
    far_copy = pltpu.make_async_remote_copy(
        src_ref=friend_low, dst_ref=far_low, send_sem=far_send, recv_sem=far_recv,
        device_id=(partner, g), device_id_type=MESH,
    )
    far_copy.start()

    for n in range(1, 12):
        loads[n].wait()
    tables = [
        (
            rate_rows[s : s + 1, :], rate_cols[s : s + 1, :], rate_counts[:, s : s + 1],
            item_tiles, user_tiles * item_tiles,
        )
        for s in range(2)
    ]
    tables.append(
        (
            trust_rows[...], trust_cols[...], trust_counts[...],
            friend_tiles, user_tiles * friend_tiles,
        )
    )
    line[...] = jnp.broadcast_to(slot_table(seats, tables, edge), line.shape)
    table_copy = pltpu.make_async_copy(line, table, table_sem)
    table_copy.start()

    def tile_rows(tile):
        return pl.ds(pl.multiple_of(tile * edge, edge), edge)

    def keep_user(rows, state):
        user_low[rows, :] = state.astype(bf16)
        user_t[:, rows] = state.T.astype(bf16)

    for tile in range(user_tiles):
        rows = pl.ds(tile * edge, edge)
        keep_user(rows, user[rows, :])
        user_acc[rows, :] = as_columns(user_accum[pl.ds(tile, 1), :], edge)
    item_low[...] = item[...].astype(bf16)
    table_copy.wait()

    def right_products(right_low, values, masks, base, col_tiles, chunk):
        columns = pl.ds(chunk * wide, wide)

        for pair in range(user_tiles // 2):
            predict = lax.dot_general(
                user_low[pl.ds(pair * wide, wide), :], right_low[columns, :],
                (((1,), (1,)), ((), ())), preferred_element_type=f32,
            )
            for i in range(2):
                for k in range(2):
                    slot = table[0, base + (2 * pair + i) * col_tiles + 2 * chunk + k]
                    seen = (spread(masks[:, pl.ds(slot, 1), :], edge) & bits[...]) != 0
                    error = (
                        values[jnp.minimum(slot, values.shape[0] - 1)].astype(f32)
                        - predict[i * edge : (i + 1) * edge, k * edge : (k + 1) * edge]
                    )
                    residual[
                        pl.ds((2 * pair + i) * edge, edge), pl.ds(chunk * wide + k * edge, edge)
                    ] = jnp.where(seen, error, 0.0).astype(bf16)
        return jnp.dot(user_t[...], residual[:, columns], preferred_element_type=f32)

    def update_users(right_low, width, finish):
        for pair in range(user_tiles // 2):
            rows = pl.ds(pair * wide, wide)
            product = jnp.dot(
                residual[rows, pl.ds(0, width)], right_low[...], preferred_element_type=f32
            )
            state = user[rows, :]
            state, accum = row_update(state, user_acc[rows, :], shrinkage * state - product)
            finish(pair, rows, state, accum)

    def part_copy(stratum, owner, source):
        return pltpu.make_async_remote_copy(
            src_ref=part[stratum].at[owner], dst_ref=gathered[stratum].at[source],
            send_sem=part_send.at[stratum, owner], recv_sem=part_recv.at[stratum, source],
            device_id=(b, owner), device_id_type=MESH,
        )

    def send_parts(stratum, right_low, values, masks, base):
        for chunk in range(item_tiles // 2):
            product = right_products(right_low, values, masks, base, item_tiles, chunk)
            for k in range(2):
                owner = 2 * chunk + k
                piece = product[:, k * edge : (k + 1) * edge].T.astype(part[stratum].dtype)
                part[stratum][owner] = piece

                @pl.when(owner != g)
                def _():
                    part_copy(stratum, owner, g).start()

                @pl.when(owner == g)
                def _():
                    gathered[stratum][g] = piece

    def part_total(stratum):
        for source in range(groups):
            @pl.when(source != g)
            def _():
                part_copy(stratum, source, source).wait_recv()

        total = gathered[stratum][0].astype(f32)
        for source in range(1, groups):
            total = total + gathered[stratum][source].astype(f32)
        return total

    loads[12].wait()
    loads[13].wait()
    send_parts(0, item_low, values_0, masks_0, 0)

    def middle_user(pair, rows, state, accum):
        user[rows, :] = state
        user_acc[rows, :] = accum
        keep_user(rows, state)

    update_users(item_low, item_rows, middle_user)

    share = item[tile_rows(g), :]
    share, share_acc = row_update(
        share, as_columns(item_accum[pl.ds(g, 1), :], edge), shrinkage * share - part_total(0)
    )
    share_low[...] = share.astype(bf16)
    low_copies = [
        pltpu.make_async_remote_copy(
            src_ref=share_low, dst_ref=item_next.at[tile_rows(g), :],
            send_sem=low_send.at[other], recv_sem=low_recv.at[g],
            device_id=(after, other), device_id_type=MESH,
        )
        for other in range(groups)
    ]
    for copy in low_copies:
        copy.start()
    ship[pl.ds(0, edge), :] = share
    ship[pl.ds(edge, 8), :] = share_acc.T[0:8, :]
    ship_copy = pltpu.make_async_remote_copy(
        src_ref=ship, dst_ref=shipped, send_sem=ship_send, recv_sem=ship_recv,
        device_id=(after, g), device_id_type=MESH,
    )
    ship_copy.start()

    for n in range(14, len(loads)):
        loads[n].wait()
    for source in range(groups):
        pltpu.make_async_remote_copy(
            src_ref=share_low, dst_ref=item_next.at[pl.ds(source * edge, edge), :],
            send_sem=low_send.at[source], recv_sem=low_recv.at[source],
            device_id=(after, source), device_id_type=MESH,
        ).wait_recv()
    send_parts(1, item_next, values_1, masks_1, user_tiles * item_tiles)
    update_users(item_next, item_rows, middle_user)

    far_copy.wait_recv()

    def back_copy(chunk):
        rows = pl.ds(chunk * wide, wide)
        return pltpu.make_async_remote_copy(
            src_ref=far_part.at[rows, :], dst_ref=friend_part.at[rows, :],
            send_sem=back_send.at[chunk], recv_sem=back_recv.at[chunk],
            device_id=(partner, g), device_id_type=MESH,
        )

    for chunk in range(friend_tiles // 2):
        product = right_products(
            far_low, values_2, masks_2, 2 * user_tiles * item_tiles, friend_tiles, chunk
        )
        far_part[pl.ds(chunk * wide, wide), :] = product.T.astype(bf16)
        back_copy(chunk).start()

    def last_user(pair, rows, state, accum):
        user_out[rows, :] = state
        for k in range(2):
            user_acc_out[pl.ds(2 * pair + k, 1), :] = accum[k * edge : (k + 1) * edge].T[0:1, :]

    update_users(far_low, friend_rows, last_user)

    ship_copy.wait_recv()
    share = shipped[pl.ds(0, edge), :]
    share_acc = as_columns(shipped[pl.ds(edge, 1), :], edge)
    share, share_acc = row_update(share, share_acc, shrinkage * share - part_total(1))
    item_out[...] = share
    item_acc_out[...] = share_acc.T[0:1, :]

    for chunk in range(friend_tiles // 2):
        back_copy(chunk).wait_recv()
        for k in range(2):
            tile = 2 * chunk + k
            rows = pl.ds(tile * edge, edge)
            state = friend[rows, :]
            gradient = shrinkage * state - friend_part[rows, :].astype(f32)
            accum = as_columns(friend_accum[pl.ds(tile, 1), :], edge)
            state, accum = row_update(state, accum, gradient)
            friend_out[rows, :] = state
            friend_acc_out[pl.ds(tile, 1), :] = accum.T[0:1, :]

    far_copy.wait_send()
    for stratum in range(2):
        for owner in range(groups):
            @pl.when(owner != g)
            def _():
                part_copy(stratum, owner, g).wait_send()
    for copy in low_copies:
        copy.wait_send()
    ship_copy.wait_send()
    for chunk in range(friend_tiles // 2):
        back_copy(chunk).wait_send()


def finish_kernel(*refs):
    count = len(refs) // 2
    copies = [
        pltpu.make_async_copy(refs[n], refs[count + n], refs[-1].at[n]) for n in range(count)
    ]
    for copy in copies:
        copy.start()
    for copy in copies:
        copy.wait()


def local(
    user_factors, user_accum, friend_factors, friend_accum, item_factors, item_accum,
    rating_values, rating_masks, rating_rows, rating_cols, rating_counts,
    trust_values, trust_masks, trust_rows, trust_cols, trust_counts,
):
    blocks, groups = lax.axis_size("blk"), lax.axis_size("grp")
    edge, rank = rating_values.shape[-1], user_factors.shape[-1]
    users, items, friends = (
        user_factors.shape[0], item_factors.shape[0], friend_factors.shape[0]
    )
    user_tiles, item_tiles, friend_tiles = users // edge, items // edge, friends // edge
    assert edge == rank and items == groups * edge and blocks > 2
    assert user_tiles % 2 == 0 and item_tiles % 2 == 0 and friend_tiles % 2 == 0
    vmem = pl.BlockSpec(memory_space=pltpu.VMEM)
    hbm = pl.BlockSpec(memory_space=pltpu.HBM)
    dma = pltpu.SemaphoreType.DMA
    flops = 6 * rank * users * (2 * items + friends)
    shapes = [
        jax.ShapeDtypeStruct((users, rank), f32),
        jax.ShapeDtypeStruct((user_tiles, edge), f32),
        jax.ShapeDtypeStruct((friends, rank), f32),
        jax.ShapeDtypeStruct((friend_tiles, edge), f32),
        jax.ShapeDtypeStruct((edge, rank), f32),
        jax.ShapeDtypeStruct((1, edge), f32),
    ]
    rate_slots, mask_words = rating_masks.shape[1:3]
    trust_slots = trust_masks.shape[0]
    results = pl.pallas_call(
        functools.partial(strata_kernel, blocks, groups),
        out_shape=shapes,
        in_specs=[hbm] * 16,
        out_specs=[vmem] * 6,
        scratch_shapes=[
            pltpu.VMEM((users, rank), f32),
            pltpu.VMEM((users, edge), f32),
            pltpu.VMEM((users, rank), bf16),
            pltpu.VMEM((rank, users), bf16),
            pltpu.VMEM((friends, rank), f32),
            pltpu.VMEM((friends, rank), bf16),
            pltpu.VMEM((friends, rank), bf16),
            pltpu.VMEM((items, rank), f32),
            pltpu.VMEM((items, rank), bf16),
            pltpu.VMEM((items, rank), bf16),
            pltpu.VMEM(rating_values.shape[1:], bf16),
            pltpu.VMEM(rating_values.shape[1:], bf16),
            pltpu.VMEM(trust_values.shape, bf16),
            pltpu.VMEM((mask_words, rate_slots + 8, edge), jnp.int32),
            pltpu.VMEM((mask_words, rate_slots + 8, edge), jnp.int32),
            pltpu.VMEM((mask_words, trust_slots + 8, edge), jnp.int32),
            pltpu.VMEM((edge, edge), jnp.int32),
            pltpu.VMEM((users, max(items, friends)), bf16),
            pltpu.VMEM((user_tiles, edge), f32),
            pltpu.VMEM((friend_tiles, edge), f32),
            pltpu.VMEM((item_tiles, edge), f32),
            pltpu.VMEM((2, rate_slots), jnp.int32),
            pltpu.VMEM((2, rate_slots), jnp.int32),
            pltpu.VMEM((1, 2), jnp.int32),
            pltpu.VMEM((1, trust_slots), jnp.int32),
            pltpu.VMEM((1, trust_slots), jnp.int32),
            pltpu.VMEM((1, 1), jnp.int32),
            pltpu.VMEM((8, edge), jnp.int32),
            pltpu.VMEM((8, edge), jnp.int32),
            pltpu.SMEM((8, edge), jnp.int32),
            pltpu.VMEM((groups, edge, rank), f32),
            pltpu.VMEM((groups, edge, rank), bf16),
            pltpu.VMEM((groups, edge, rank), f32),
            pltpu.VMEM((groups, edge, rank), bf16),
            pltpu.VMEM((edge, rank), bf16),
            pltpu.VMEM((edge + 8, rank), f32),
            pltpu.VMEM((edge + 8, rank), f32),
            pltpu.VMEM((friends, rank), bf16),
            pltpu.VMEM((friends, rank), bf16),
            dma((18,)), dma,
            dma, dma,
            dma((2, groups)), dma((2, groups)),
            dma((groups,)), dma((groups,)),
            dma, dma,
            dma((friend_tiles // 2,)), dma((friend_tiles // 2,)),
        ],
        compiler_params=pltpu.CompilerParams(
            collective_id=0, has_side_effects=True, vmem_limit_bytes=58 * 1024 * 1024
        ),
        cost_estimate=pl.CostEstimate(
            flops=flops, bytes_accessed=8 * 1024 * 1024, transcendentals=0
        ),
        name="strata",
    )(
        user_factors, friend_factors, item_factors,
        user_accum.reshape(user_tiles, edge),
        friend_accum.reshape(friend_tiles, edge),
        item_accum.reshape(item_tiles, edge),
        rating_rows, rating_cols, rating_counts.T,
        trust_rows.reshape(1, -1), trust_cols.reshape(1, -1), trust_counts.reshape(1, 1),
        rating_values, rating_masks.transpose(0, 2, 1, 3),
        trust_values, trust_masks.transpose(1, 0, 2),
    )
    results = pl.pallas_call(
        finish_kernel,
        out_shape=shapes,
        in_specs=[hbm] * len(shapes),
        out_specs=[hbm] * len(shapes),
        scratch_shapes=[dma((len(shapes),))],
        compiler_params=pltpu.CompilerParams(vmem_limit_bytes=58 * 1024 * 1024),
        name="finish",
    )(*results)
    return tuple(
        result.reshape(-1) if n % 2 else result for n, result in enumerate(results)
    )


def solution(mesh):
    split = P(("blk", "grp"))
    second = P(None, ("blk", "grp"))
    return jax.shard_map(
        local,
        mesh=mesh,
        in_specs=(
            split, split, split, split, P("blk"), P("blk"),
            second, second, second, second, second,
            split, split, split, split, split,
        ),
        out_specs=(split,) * 6,
        check_vma=False,
    )
```

```python
import functools

import jax
import jax.numpy as jnp
from jax import lax
from jax.experimental import pallas as pl
from jax.experimental.pallas import tpu as pltpu
from jax.sharding import PartitionSpec as P

learn_rate = 0.3
shrinkage = 0.02
word_bits = 14
MESH = pl.DeviceIdType.MESH
f32, bf16 = jnp.float32, jnp.bfloat16


def slot_table(seats, tables, edge):
    seats[...] = jnp.full_like(seats[...], -2 * edge)
    for n, (rows, cols, count, across, _) in enumerate(tables):
        place = rows * across + cols
        slot = lax.broadcasted_iota(jnp.int32, place.shape, 1)
        seats[n : n + 1, 0 : place.shape[1]] = jnp.where(slot < count, place, -2 * edge)
    lane = lax.broadcasted_iota(jnp.int32, (edge, edge), 1)
    sub = lax.broadcasted_iota(jnp.int32, (edge, edge), 0)
    line = jnp.zeros((1, edge), jnp.int32)
    base = 0
    for n, (rows, _, _, _, places) in enumerate(tables):
        hit = as_columns(seats[n : n + 1, :], edge) == lane - base
        found = jnp.sum(jnp.where(hit, sub + 1, 0), axis=0, keepdims=True)
        entry = jnp.where(found > 0, found - 1, rows.shape[1])
        inside = (lane[0:1] >= base) & (lane[0:1] < base + places)
        line = jnp.where(inside, entry, line)
        base += places
    assert base <= edge
    return line


def spread(words, edge):
    sub = lax.broadcasted_iota(jnp.int32, (8, words.shape[2]), 0)
    pieces = []
    for first in range(0, edge, 8):
        low, high = first // word_bits, (first + 7) // word_bits
        piece = jnp.broadcast_to(words[low], sub.shape)
        if high != low:
            after = jnp.broadcast_to(words[high], sub.shape)
            piece = jnp.where(sub < high * word_bits - first, piece, after)
        pieces.append(piece)
    return jnp.concatenate(pieces, axis=0)


def as_columns(row, edge):
    return jnp.broadcast_to(row, (edge, edge)).T


def row_update(factor, accum, gradient):
    new_accum = accum + jnp.mean(gradient * gradient, axis=-1, keepdims=True)
    return factor - learn_rate * gradient * lax.rsqrt(new_accum), new_accum


def strata_kernel(
    blocks, groups,
    user_hbm, friend_hbm, item_hbm, user_accum_hbm, friend_accum_hbm, item_accum_hbm,
    rate_rows_hbm, rate_cols_hbm, rate_counts_hbm,
    trust_rows_hbm, trust_cols_hbm, trust_counts_hbm,
    rate_values, rate_masks, trust_values, trust_masks,
    user_out, user_acc_out, friend_out, friend_acc_out, item_out, item_acc_out,
    user, user_acc, user_low, user_t, friend, friend_low, far_low, item, item_low, item_next,
    values_0, values_1, values_2, masks_0, masks_1, masks_2, bits,
    residual, residual_1, residual_2, observed_1, observed_2, friend_acc,
    user_accum, friend_accum, item_accum,
    rate_rows, rate_cols, rate_counts, trust_rows, trust_cols, trust_counts,
    seats, line, table, part_0, part_1, gathered_0, gathered_1, share_low, ship, shipped, far_part, friend_part,
    load_sem, table_sem, far_send, far_recv, part_send, part_recv, low_send, low_recv,
    ship_send, ship_recv, back_send, back_recv,
):
    b, g = lax.axis_index("blk"), lax.axis_index("grp")
    after = lax.rem(b + 1, blocks)
    before = lax.rem(b + blocks - 1, blocks)
    partner = lax.rem(b + blocks // 2, blocks)
    edge = bits.shape[0]
    wide = 2 * edge
    user_tiles, item_tiles, friend_tiles = (
        rows.shape[0] // edge for rows in (user, item, friend)
    )

    barrier = pltpu.get_barrier_semaphore()
    for step in range(1, groups):
        pl.semaphore_signal(
            barrier, inc=1, device_id=(b, lax.rem(g + step, groups)), device_id_type=MESH
        )
    for other in range(groups):
        pl.semaphore_signal(barrier, inc=1, device_id=(before, other), device_id_type=MESH)
    pl.semaphore_signal(barrier, inc=1, device_id=(partner, g), device_id_type=MESH)

    part, gathered = (part_0, part_1), (gathered_0, gathered_1)
    rate_slots, trust_slots = values_0.shape[0], values_2.shape[0]
    pairs = [
        (rate_rows_hbm, rate_rows), (rate_cols_hbm, rate_cols), (rate_counts_hbm, rate_counts),
        (trust_rows_hbm, trust_rows), (trust_cols_hbm, trust_cols),
        (trust_counts_hbm, trust_counts),
        (user_accum_hbm, user_accum), (friend_accum_hbm, friend_accum),
        (item_accum_hbm, item_accum),
        (user_hbm, user), (item_hbm, item),
        (rate_masks.at[0], masks_0.at[:, pl.ds(0, rate_slots), :]),
        (rate_values.at[0], values_0),
        (friend_hbm, friend),
        (rate_masks.at[1], masks_1.at[:, pl.ds(0, rate_slots), :]),
        (rate_values.at[1], values_1),
        (trust_masks, masks_2.at[:, pl.ds(0, trust_slots), :]),
        (trust_values, values_2),
    ]
    loads = [
        pltpu.make_async_copy(src, dst, load_sem.at[n]) for n, (src, dst) in enumerate(pairs)
    ]
    for load in loads:
        load.start()

    place = lax.broadcasted_iota(jnp.int32, bits.shape, 0)
    bits[...] = jnp.left_shift(jnp.ones_like(place), lax.rem(place, word_bits))

    for masks in (masks_0, masks_1, masks_2):
        spare = masks.shape[1] - 8
        masks[:, pl.ds(spare, 8), :] = jnp.zeros((masks.shape[0], 8, edge), jnp.int32)

    far_copy = pltpu.make_async_remote_copy(
        src_ref=friend_low, dst_ref=far_low, send_sem=far_send, recv_sem=far_recv,
        device_id=(partner, g), device_id_type=MESH,
    )

    for n in range(11):
        loads[n].wait()
    tables = [
        (
            rate_rows[s : s + 1, :], rate_cols[s : s + 1, :], rate_counts[:, s : s + 1],
            item_tiles, user_tiles * item_tiles,
        )
        for s in range(2)
    ]
    tables.append(
        (
            trust_rows[...], trust_cols[...], trust_counts[...],
            friend_tiles, user_tiles * friend_tiles,
        )
    )
    line[...] = jnp.broadcast_to(slot_table(seats, tables, edge), line.shape)
    table_copy = pltpu.make_async_copy(line, table, table_sem)
    table_copy.start()

    def tile_rows(tile):
        return pl.ds(pl.multiple_of(tile * edge, edge), edge)

    def keep_user(rows, state):
        user_low[rows, :] = state.astype(bf16)
        user_t[:, rows] = state.T.astype(bf16)

    for tile in range(user_tiles):
        rows = pl.ds(tile * edge, edge)
        keep_user(rows, user[rows, :])
        user_acc[rows, :] = as_columns(user_accum[pl.ds(tile, 1), :], edge)
    item_low[...] = item[...].astype(bf16)
    table_copy.wait()

    def tile_operands(values, masks, index):
        slot = table[0, index]
        seen = (spread(masks[:, pl.ds(slot, 1), :], edge) & bits[...]) != 0
        return seen, values[jnp.minimum(slot, values.shape[0] - 1)]

    def prepare(held, observed, values, masks, base, col_tiles):
        for r in range(user_tiles):
            for c in range(col_tiles):
                seen, value = tile_operands(values, masks, base + r * col_tiles + c)
                at = pl.ds(r * edge, edge), pl.ds(c * edge, edge)
                held[at] = jnp.where(seen, value.astype(f32), 0.0).astype(bf16)
                observed[at] = jnp.where(seen, 1.0, 0.0).astype(bf16)

    def predicted(right_low, pair, columns):
        return lax.dot_general(
            user_low[pl.ds(pair * wide, wide), :], right_low[columns, :],
            (((1,), (1,)), ((), ())), preferred_element_type=f32,
        )

    def direct_residual(right_low, values, masks, base, col_tiles, chunk):
        for pair in range(user_tiles // 2):
            predict = predicted(right_low, pair, pl.ds(chunk * wide, wide))
            for i in range(2):
                for k in range(2):
                    seen, value = tile_operands(
                        values, masks, base + (2 * pair + i) * col_tiles + 2 * chunk + k
                    )
                    error = value.astype(f32) - (
                        predict[i * edge : (i + 1) * edge, k * edge : (k + 1) * edge]
                    )
                    residual[
                        pl.ds((2 * pair + i) * edge, edge), pl.ds(chunk * wide + k * edge, edge)
                    ] = jnp.where(seen, error, 0.0).astype(bf16)

    def prepared_residual(right_low, observed, held, chunk):
        columns = pl.ds(chunk * wide, wide)
        for pair in range(user_tiles // 2):
            rows = pl.ds(pair * wide, wide)
            predict = predicted(right_low, pair, columns)
            held[rows, columns] = (
                held[rows, columns].astype(f32) - observed[rows, columns].astype(f32) * predict
            ).astype(bf16)

    def right_products(held, chunk):
        return jnp.dot(
            user_t[...], held[:, pl.ds(chunk * wide, wide)], preferred_element_type=f32
        )

    def update_users(right_low, held, finish):
        for pair in range(user_tiles // 2):
            rows = pl.ds(pair * wide, wide)
            product = jnp.dot(
                held[rows, :], right_low[...], preferred_element_type=f32
            )
            state = user[rows, :]
            state, accum = row_update(state, user_acc[rows, :], shrinkage * state - product)
            finish(pair, rows, state, accum)

    def part_copy(stratum, owner, source):
        return pltpu.make_async_remote_copy(
            src_ref=part[stratum].at[owner], dst_ref=gathered[stratum].at[source],
            send_sem=part_send.at[stratum, owner], recv_sem=part_recv.at[stratum, source],
            device_id=(b, owner), device_id_type=MESH,
        )

    def send_parts(stratum, held, chunk):
        product = right_products(held, chunk)
        for k in range(2):
            owner = 2 * chunk + k
            piece = product[:, k * edge : (k + 1) * edge].T.astype(part[stratum].dtype)
            part[stratum][owner] = piece

            @pl.when(owner != g)
            def _():
                part_copy(stratum, owner, g).start()

            @pl.when(owner == g)
            def _():
                gathered[stratum][g] = piece

    def part_total(stratum):
        for source in range(groups):
            @pl.when(source != g)
            def _():
                part_copy(stratum, source, source).wait_recv()

        total = gathered[stratum][0].astype(f32)
        for source in range(1, groups):
            total = total + gathered[stratum][source].astype(f32)
        return total

    loads[11].wait()
    loads[12].wait()
    for chunk in range(item_tiles // 2):
        direct_residual(item_low, values_0, masks_0, 0, item_tiles, chunk)
        if chunk == 0:
            pl.semaphore_wait(barrier, 2 * groups)
        send_parts(0, residual, chunk)

    loads[13].wait()
    friend_low[...] = friend[...].astype(bf16)
    far_copy.start()

    def middle_user(pair, rows, state, accum):
        user[rows, :] = state
        user_acc[rows, :] = accum
        keep_user(rows, state)

    update_users(item_low, residual, middle_user)
    loads[14].wait()
    loads[15].wait()
    prepare(residual_1, observed_1, values_1, masks_1, user_tiles * item_tiles, item_tiles)

    share = item[tile_rows(g), :]
    share, share_acc = row_update(
        share, as_columns(item_accum[pl.ds(g, 1), :], edge), shrinkage * share - part_total(0)
    )
    share_low[...] = share.astype(bf16)
    low_copies = [
        pltpu.make_async_remote_copy(
            src_ref=share_low, dst_ref=item_next.at[tile_rows(g), :],
            send_sem=low_send.at[other], recv_sem=low_recv.at[g],
            device_id=(after, other), device_id_type=MESH,
        )
        for other in range(groups)
    ]
    for copy in low_copies:
        copy.start()
    ship[pl.ds(0, edge), :] = share
    ship[pl.ds(edge, 8), :] = share_acc.T[0:8, :]
    ship_copy = pltpu.make_async_remote_copy(
        src_ref=ship, dst_ref=shipped, send_sem=ship_send, recv_sem=ship_recv,
        device_id=(after, g), device_id_type=MESH,
    )
    ship_copy.start()

    loads[16].wait()
    loads[17].wait()
    prepare(
        residual_2, observed_2, values_2, masks_2, 2 * user_tiles * item_tiles, friend_tiles
    )
    for tile in range(friend_tiles):
        friend_acc[pl.ds(tile * edge, edge), :] = as_columns(
            friend_accum[pl.ds(tile, 1), :], edge
        )
    for source in range(groups):
        pltpu.make_async_remote_copy(
            src_ref=share_low, dst_ref=item_next.at[pl.ds(source * edge, edge), :],
            send_sem=low_send.at[source], recv_sem=low_recv.at[source],
            device_id=(after, source), device_id_type=MESH,
        ).wait_recv()
    for chunk in range(item_tiles // 2):
        prepared_residual(item_next, observed_1, residual_1, chunk)
        send_parts(1, residual_1, chunk)
    update_users(item_next, residual_1, middle_user)

    far_copy.wait_recv()

    def back_copy(chunk):
        rows = pl.ds(chunk * wide, wide)
        return pltpu.make_async_remote_copy(
            src_ref=far_part.at[rows, :], dst_ref=friend_part.at[rows, :],
            send_sem=back_send.at[chunk], recv_sem=back_recv.at[chunk],
            device_id=(partner, g), device_id_type=MESH,
        )

    for chunk in range(friend_tiles // 2):
        prepared_residual(far_low, observed_2, residual_2, chunk)
        product = right_products(residual_2, chunk)
        far_part[pl.ds(chunk * wide, wide), :] = product.T.astype(bf16)
        back_copy(chunk).start()

    def last_user(pair, rows, state, accum):
        user_out[rows, :] = state
        for k in range(2):
            user_acc_out[pl.ds(2 * pair + k, 1), :] = accum[k * edge : (k + 1) * edge].T[0:1, :]

    update_users(far_low, residual_2, last_user)

    ship_copy.wait_recv()
    share = shipped[pl.ds(0, edge), :]
    share_acc = as_columns(shipped[pl.ds(edge, 1), :], edge)
    share, share_acc = row_update(share, share_acc, shrinkage * share - part_total(1))
    item_out[...] = share
    item_acc_out[...] = share_acc.T[0:1, :]

    for chunk in range(friend_tiles // 2):
        back_copy(chunk).wait_recv()
        for k in range(2):
            tile = 2 * chunk + k
            rows = pl.ds(tile * edge, edge)
            state = friend[rows, :]
            gradient = shrinkage * state - friend_part[rows, :].astype(f32)
            state, accum = row_update(state, friend_acc[rows, :], gradient)
            friend_out[rows, :] = state
            friend_acc_out[pl.ds(tile, 1), :] = accum.T[0:1, :]

    far_copy.wait_send()
    for stratum in range(2):
        for owner in range(groups):
            @pl.when(owner != g)
            def _():
                part_copy(stratum, owner, g).wait_send()
    for copy in low_copies:
        copy.wait_send()
    ship_copy.wait_send()
    for chunk in range(friend_tiles // 2):
        back_copy(chunk).wait_send()


def finish_kernel(count, *refs):
    sources, targets, held = refs[:count], refs[count : 2 * count], refs[2 * count : -2]
    fills = [
        pltpu.make_async_copy(sources[n], held[n], refs[-2].at[n]) for n in range(count)
    ]
    drains = [
        pltpu.make_async_copy(held[n], targets[n], refs[-1].at[n]) for n in range(count)
    ]
    for copy in fills:
        copy.start()
    for fill, drain in zip(fills, drains):
        fill.wait()
        drain.start()
    for copy in drains:
        copy.wait()


def local(
    user_factors, user_accum, friend_factors, friend_accum, item_factors, item_accum,
    rating_values, rating_masks, rating_rows, rating_cols, rating_counts,
    trust_values, trust_masks, trust_rows, trust_cols, trust_counts,
):
    blocks, groups = lax.axis_size("blk"), lax.axis_size("grp")
    edge, rank = rating_values.shape[-1], user_factors.shape[-1]
    users, items, friends = (
        user_factors.shape[0], item_factors.shape[0], friend_factors.shape[0]
    )
    user_tiles, item_tiles, friend_tiles = users // edge, items // edge, friends // edge
    assert edge == rank and items == groups * edge and blocks > 2
    assert user_tiles % 2 == 0 and item_tiles % 2 == 0 and friend_tiles % 2 == 0
    vmem = pl.BlockSpec(memory_space=pltpu.VMEM)
    hbm = pl.BlockSpec(memory_space=pltpu.HBM)
    dma = pltpu.SemaphoreType.DMA
    flops = 6 * rank * users * (2 * items + friends)
    shapes = [
        jax.ShapeDtypeStruct((users, rank), f32),
        jax.ShapeDtypeStruct((user_tiles, edge), f32),
        jax.ShapeDtypeStruct((friends, rank), f32),
        jax.ShapeDtypeStruct((friend_tiles, edge), f32),
        jax.ShapeDtypeStruct((edge, rank), f32),
        jax.ShapeDtypeStruct((1, edge), f32),
    ]
    rate_slots, mask_words = rating_masks.shape[1:3]
    trust_slots = trust_masks.shape[0]
    results = pl.pallas_call(
        functools.partial(strata_kernel, blocks, groups),
        out_shape=shapes,
        in_specs=[hbm] * 16,
        out_specs=[vmem] * 6,
        scratch_shapes=[
            pltpu.VMEM((users, rank), f32),
            pltpu.VMEM((users, edge), f32),
            pltpu.VMEM((users, rank), bf16),
            pltpu.VMEM((rank, users), bf16),
            pltpu.VMEM((friends, rank), f32),
            pltpu.VMEM((friends, rank), bf16),
            pltpu.VMEM((friends, rank), bf16),
            pltpu.VMEM((items, rank), f32),
            pltpu.VMEM((items, rank), bf16),
            pltpu.VMEM((items, rank), bf16),
            pltpu.VMEM(rating_values.shape[1:], bf16),
            pltpu.VMEM(rating_values.shape[1:], bf16),
            pltpu.VMEM(trust_values.shape, bf16),
            pltpu.VMEM((mask_words, rate_slots + 8, edge), jnp.int32),
            pltpu.VMEM((mask_words, rate_slots + 8, edge), jnp.int32),
            pltpu.VMEM((mask_words, trust_slots + 8, edge), jnp.int32),
            pltpu.VMEM((edge, edge), jnp.int32),
            pltpu.VMEM((users, items), bf16),
            pltpu.VMEM((users, items), bf16),
            pltpu.VMEM((users, friends), bf16),
            pltpu.VMEM((users, items), bf16),
            pltpu.VMEM((users, friends), bf16),
            pltpu.VMEM((friends, edge), f32),
            pltpu.VMEM((user_tiles, edge), f32),
            pltpu.VMEM((friend_tiles, edge), f32),
            pltpu.VMEM((item_tiles, edge), f32),
            pltpu.VMEM((2, rate_slots), jnp.int32),
            pltpu.VMEM((2, rate_slots), jnp.int32),
            pltpu.VMEM((1, 2), jnp.int32),
            pltpu.VMEM((1, trust_slots), jnp.int32),
            pltpu.VMEM((1, trust_slots), jnp.int32),
            pltpu.VMEM((1, 1), jnp.int32),
            pltpu.VMEM((8, edge), jnp.int32),
            pltpu.VMEM((8, edge), jnp.int32),
            pltpu.SMEM((8, edge), jnp.int32),
            pltpu.VMEM((groups, edge, rank), f32),
            pltpu.VMEM((groups, edge, rank), bf16),
            pltpu.VMEM((groups, edge, rank), f32),
            pltpu.VMEM((groups, edge, rank), bf16),
            pltpu.VMEM((edge, rank), bf16),
            pltpu.VMEM((edge + 8, rank), f32),
            pltpu.VMEM((edge + 8, rank), f32),
            pltpu.VMEM((friends, rank), bf16),
            pltpu.VMEM((friends, rank), bf16),
            dma((18,)), dma,
            dma, dma,
            dma((2, groups)), dma((2, groups)),
            dma((groups,)), dma((groups,)),
            dma, dma,
            dma((friend_tiles // 2,)), dma((friend_tiles // 2,)),
        ],
        compiler_params=pltpu.CompilerParams(
            collective_id=0, has_side_effects=True, vmem_limit_bytes=58 * 1024 * 1024
        ),
        cost_estimate=pl.CostEstimate(
            flops=flops, bytes_accessed=8 * 1024 * 1024, transcendentals=0
        ),
        name="strata",
    )(
        user_factors, friend_factors, item_factors,
        user_accum.reshape(user_tiles, edge),
        friend_accum.reshape(friend_tiles, edge),
        item_accum.reshape(item_tiles, edge),
        rating_rows, rating_cols, rating_counts.T,
        trust_rows.reshape(1, -1), trust_cols.reshape(1, -1), trust_counts.reshape(1, 1),
        rating_values, rating_masks.transpose(0, 2, 1, 3),
        trust_values, trust_masks.transpose(1, 0, 2),
    )
    results = pl.pallas_call(
        functools.partial(finish_kernel, len(shapes)),
        out_shape=shapes,
        in_specs=[hbm] * len(shapes),
        out_specs=[hbm] * len(shapes),
        scratch_shapes=[pltpu.VMEM(shape.shape, shape.dtype) for shape in shapes]
        + [dma((len(shapes),)), dma((len(shapes),))],
        compiler_params=pltpu.CompilerParams(vmem_limit_bytes=58 * 1024 * 1024),
        name="finish",
    )(*results)
    return tuple(
        result.reshape(-1) if n % 2 else result for n, result in enumerate(results)
    )


def solution(mesh):
    split = P(("blk", "grp"))
    second = P(None, ("blk", "grp"))
    return jax.shard_map(
        local,
        mesh=mesh,
        in_specs=(
            split, split, split, split, P("blk"), P("blk"),
            second, second, second, second, second,
            split, split, split, split, split,
        ),
        out_specs=(split,) * 6,
        check_vma=False,
    )
```

```python
import functools

import jax
import jax.numpy as jnp
from jax import lax
from jax.experimental import pallas as pl
from jax.experimental.pallas import tpu as pltpu
from jax.sharding import PartitionSpec as P

learn_rate = 0.3
shrinkage = 0.02
word_bits = 14
MESH = pl.DeviceIdType.MESH
f32, bf16 = jnp.float32, jnp.bfloat16


def slot_table(seats, tables, edge):
    seats[...] = jnp.full_like(seats[...], -2 * edge)
    for n, (rows, cols, count, across, _) in enumerate(tables):
        place = rows * across + cols
        slot = lax.broadcasted_iota(jnp.int32, place.shape, 1)
        seats[n : n + 1, 0 : place.shape[1]] = jnp.where(slot < count, place, -2 * edge)
    lane = lax.broadcasted_iota(jnp.int32, (edge, edge), 1)
    sub = lax.broadcasted_iota(jnp.int32, (edge, edge), 0)
    line = jnp.zeros((1, edge), jnp.int32)
    base = 0
    for n, (rows, _, _, _, places) in enumerate(tables):
        hit = as_columns(seats[n : n + 1, :], edge) == lane - base
        found = jnp.sum(jnp.where(hit, sub + 1, 0), axis=0, keepdims=True)
        entry = jnp.where(found > 0, found - 1, rows.shape[1])
        inside = (lane[0:1] >= base) & (lane[0:1] < base + places)
        line = jnp.where(inside, entry, line)
        base += places
    assert base <= edge
    return line


def spread(words, edge):
    sub = lax.broadcasted_iota(jnp.int32, (8, words.shape[2]), 0)
    pieces = []
    for first in range(0, edge, 8):
        low, high = first // word_bits, (first + 7) // word_bits
        piece = jnp.broadcast_to(words[low], sub.shape)
        if high != low:
            after = jnp.broadcast_to(words[high], sub.shape)
            piece = jnp.where(sub < high * word_bits - first, piece, after)
        pieces.append(piece)
    return jnp.concatenate(pieces, axis=0)


def as_columns(row, edge):
    return jnp.broadcast_to(row, (edge, edge)).T


def row_update(factor, accum, gradient):
    new_accum = accum + jnp.mean(gradient * gradient, axis=-1, keepdims=True)
    return factor - learn_rate * gradient * lax.rsqrt(new_accum), new_accum


def strata_kernel(
    blocks, groups,
    user_hbm, friend_hbm, item_hbm, user_accum_hbm, friend_accum_hbm, item_accum_hbm,
    rate_rows_hbm, rate_cols_hbm, rate_counts_hbm,
    trust_rows_hbm, trust_cols_hbm, trust_counts_hbm,
    rate_values, rate_masks, trust_values, trust_masks,
    user_out, user_acc_out, friend_out, friend_acc_out, item_out, item_acc_out,
    user, user_acc, user_low, user_t, user_t_last, friend, friend_low, far_low, item, item_low, item_next,
    values_0, values_1, values_2, masks_0, masks_1, masks_2, bits,
    residual, residual_1, residual_2, observed_1, observed_2, friend_acc,
    user_accum, friend_accum, item_accum,
    rate_rows, rate_cols, rate_counts, trust_rows, trust_cols, trust_counts,
    seats, line, table, part_0, part_1, gathered_0, gathered_1, share_end, share_acc_end,
    share_low, ship, shipped, far_part, friend_part,
    load_sem, store_sem, table_sem, far_send, far_recv, part_send, part_recv, low_send, low_recv,
    ship_send, ship_recv, back_send, back_recv,
):
    b, g = lax.axis_index("blk"), lax.axis_index("grp")
    after = lax.rem(b + 1, blocks)
    before = lax.rem(b + blocks - 1, blocks)
    partner = lax.rem(b + blocks // 2, blocks)
    edge = bits.shape[0]
    wide = 2 * edge
    user_tiles, item_tiles, friend_tiles = (
        rows.shape[0] // edge for rows in (user, item, friend)
    )

    barrier = pltpu.get_barrier_semaphore()
    for step in range(1, groups):
        pl.semaphore_signal(
            barrier, inc=1, device_id=(b, lax.rem(g + step, groups)), device_id_type=MESH
        )
    for other in range(groups):
        pl.semaphore_signal(barrier, inc=1, device_id=(before, other), device_id_type=MESH)
    pl.semaphore_signal(barrier, inc=1, device_id=(partner, g), device_id_type=MESH)

    part, gathered = (part_0, part_1), (gathered_0, gathered_1)
    rate_slots, trust_slots = values_0.shape[0], values_2.shape[0]
    pairs = [
        (rate_rows_hbm, rate_rows), (rate_cols_hbm, rate_cols), (rate_counts_hbm, rate_counts),
        (trust_rows_hbm, trust_rows), (trust_cols_hbm, trust_cols),
        (trust_counts_hbm, trust_counts),
        (user_accum_hbm, user_accum), (friend_accum_hbm, friend_accum),
        (item_accum_hbm, item_accum),
        (user_hbm, user), (item_hbm, item),
        (rate_masks.at[0], masks_0.at[:, pl.ds(0, rate_slots), :]),
        (rate_values.at[0], values_0),
        (friend_hbm, friend),
        (rate_masks.at[1], masks_1.at[:, pl.ds(0, rate_slots), :]),
        (rate_values.at[1], values_1),
        (trust_masks, masks_2.at[:, pl.ds(0, trust_slots), :]),
        (trust_values, values_2),
    ]
    loads = [
        pltpu.make_async_copy(src, dst, load_sem.at[n]) for n, (src, dst) in enumerate(pairs)
    ]
    for load in loads[:13]:
        load.start()

    place = lax.broadcasted_iota(jnp.int32, bits.shape, 0)
    bits[...] = jnp.left_shift(jnp.ones_like(place), lax.rem(place, word_bits))

    for masks in (masks_0, masks_1, masks_2):
        spare = masks.shape[1] - 8
        masks[:, pl.ds(spare, 8), :] = jnp.zeros((masks.shape[0], 8, edge), jnp.int32)

    far_copy = pltpu.make_async_remote_copy(
        src_ref=friend_low, dst_ref=far_low, send_sem=far_send, recv_sem=far_recv,
        device_id=(partner, g), device_id_type=MESH,
    )

    for n in range(11):
        loads[n].wait()
    tables = [
        (
            rate_rows[s : s + 1, :], rate_cols[s : s + 1, :], rate_counts[:, s : s + 1],
            item_tiles, user_tiles * item_tiles,
        )
        for s in range(2)
    ]
    tables.append(
        (
            trust_rows[...], trust_cols[...], trust_counts[...],
            friend_tiles, user_tiles * friend_tiles,
        )
    )
    line[...] = jnp.broadcast_to(slot_table(seats, tables, edge), line.shape)
    table_copy = pltpu.make_async_copy(line, table, table_sem)
    table_copy.start()

    def tile_rows(tile):
        return pl.ds(pl.multiple_of(tile * edge, edge), edge)

    def keep_user(target_t, rows, state):
        user_low[rows, :] = state.astype(bf16)
        target_t[:, rows] = state.T.astype(bf16)

    for tile in range(user_tiles):
        rows = pl.ds(tile * edge, edge)
        keep_user(user_t, rows, user[rows, :])
        user_acc[rows, :] = as_columns(user_accum[pl.ds(tile, 1), :], edge)
    item_low[...] = item[...].astype(bf16)
    table_copy.wait()

    def tile_operands(values, masks, index):
        slot = table[0, index]
        seen = (spread(masks[:, pl.ds(slot, 1), :], edge) & bits[...]) != 0
        return seen, values[jnp.minimum(slot, values.shape[0] - 1)]

    def wide_columns(chunk):
        return pl.ds(pl.multiple_of(chunk * wide, wide), wide)

    def prepare(held, observed, values, masks, base, col_tiles):
        for r in range(user_tiles):
            for c in range(col_tiles):
                seen, value = tile_operands(values, masks, base + r * col_tiles + c)
                at = pl.ds(r * edge, edge), pl.ds(c * edge, edge)
                held[at] = jnp.where(seen, value.astype(f32), 0.0).astype(bf16)
                observed[at] = jnp.where(seen, 1.0, 0.0).astype(bf16)

    def predicted(right_low, pair, columns):
        return lax.dot_general(
            user_low[pl.ds(pair * wide, wide), :], right_low[columns, :],
            (((1,), (1,)), ((), ())), preferred_element_type=f32,
        )

    def direct_residual(right_low, values, masks, base, col_tiles, chunk):
        for pair in range(user_tiles // 2):
            predict = predicted(right_low, pair, wide_columns(chunk))
            for i in range(2):
                for k in range(2):
                    seen, value = tile_operands(
                        values, masks, base + (2 * pair + i) * col_tiles + 2 * chunk + k
                    )
                    error = value.astype(f32) - (
                        predict[i * edge : (i + 1) * edge, k * edge : (k + 1) * edge]
                    )
                    residual[
                        pl.ds((2 * pair + i) * edge, edge),
                        pl.ds(pl.multiple_of(chunk * wide + k * edge, edge), edge),
                    ] = jnp.where(seen, error, 0.0).astype(bf16)

    def prepared_residual(right_low, observed, held, chunk):
        columns = wide_columns(chunk)
        for pair in range(user_tiles // 2):
            rows = pl.ds(pair * wide, wide)
            predict = predicted(right_low, pair, columns)
            held[rows, columns] = (
                held[rows, columns].astype(f32) - observed[rows, columns].astype(f32) * predict
            ).astype(bf16)

    def right_products(left_t, held, chunk):
        return jnp.dot(
            left_t[...], held[:, wide_columns(chunk)], preferred_element_type=f32
        )

    def update_users(right_low, held, finish):
        for pair in range(user_tiles // 2):
            rows = pl.ds(pair * wide, wide)
            product = jnp.dot(
                held[rows, :], right_low[...], preferred_element_type=f32
            )
            state = user[rows, :]
            state, accum = row_update(state, user_acc[rows, :], shrinkage * state - product)
            finish(pair, rows, state, accum)

    def part_copy(stratum, owner, source):
        return pltpu.make_async_remote_copy(
            src_ref=part[stratum].at[owner], dst_ref=gathered[stratum].at[source],
            send_sem=part_send.at[stratum, owner], recv_sem=part_recv.at[stratum, source],
            device_id=(b, owner), device_id_type=MESH,
        )

    def send_parts(stratum, left_t, held, chunk):
        product = right_products(left_t, held, chunk)
        for k in range(2):
            owner = 2 * chunk + k
            piece = product[:, k * edge : (k + 1) * edge].T.astype(part[stratum].dtype)
            part[stratum][owner] = piece

            @pl.when(owner != g)
            def _():
                part_copy(stratum, owner, g).start()

            @pl.when(owner == g)
            def _():
                gathered[stratum][g] = piece

    def part_total(stratum):
        for source in range(groups):
            @pl.when(source != g)
            def _():
                part_copy(stratum, source, source).wait_recv()

        total = gathered[stratum][0].astype(f32)
        for source in range(1, groups):
            total = total + gathered[stratum][source].astype(f32)
        return total

    loads[11].wait()
    loads[12].wait()
    for load in loads[13:]:
        load.start()
    chunks = item_tiles // 2
    near = lax.div(g, 2)
    for step in range(chunks):
        chunk = lax.rem(near + 1 + step, chunks)
        direct_residual(item_low, values_0, masks_0, 0, item_tiles, chunk)
        if step == 0:
            pl.semaphore_wait(barrier, 2 * groups)
        send_parts(0, user_t, residual, chunk)

    loads[13].wait()
    friend_low[...] = friend[...].astype(bf16)
    far_copy.start()

    def middle_user(target_t):
        def finish(pair, rows, state, accum):
            user[rows, :] = state
            user_acc[rows, :] = accum
            keep_user(target_t, rows, state)

        return finish

    update_users(item_low, residual, middle_user(user_t))
    loads[14].wait()
    loads[15].wait()
    prepare(residual_1, observed_1, values_1, masks_1, user_tiles * item_tiles, item_tiles)

    share = item[tile_rows(g), :]
    share, share_acc = row_update(
        share, as_columns(item_accum[pl.ds(g, 1), :], edge), shrinkage * share - part_total(0)
    )
    share_low[...] = share.astype(bf16)
    low_copies = [
        pltpu.make_async_remote_copy(
            src_ref=share_low, dst_ref=item_next.at[tile_rows(g), :],
            send_sem=low_send.at[step], recv_sem=low_recv.at[g],
            device_id=(after, lax.rem(g + groups // 2 + step, groups)), device_id_type=MESH,
        )
        for step in range(groups)
    ]
    for copy in low_copies:
        copy.start()
    ship[pl.ds(0, edge), :] = share
    ship[pl.ds(edge, 8), :] = share_acc.T[0:8, :]
    ship_copy = pltpu.make_async_remote_copy(
        src_ref=ship, dst_ref=shipped, send_sem=ship_send, recv_sem=ship_recv,
        device_id=(after, g), device_id_type=MESH,
    )
    ship_copy.start()

    loads[16].wait()
    loads[17].wait()
    prepare(
        residual_2, observed_2, values_2, masks_2, 2 * user_tiles * item_tiles, friend_tiles
    )
    for tile in range(friend_tiles):
        friend_acc[pl.ds(tile * edge, edge), :] = as_columns(
            friend_accum[pl.ds(tile, 1), :], edge
        )
    for step in range(chunks):
        chunk = lax.rem(near + step, chunks)
        for k in range(2):
            source = 2 * chunk + k
            pltpu.make_async_remote_copy(
                src_ref=share_low, dst_ref=item_next.at[tile_rows(source), :],
                send_sem=low_send.at[source], recv_sem=low_recv.at[source],
                device_id=(after, source), device_id_type=MESH,
            ).wait_recv()
        prepared_residual(item_next, observed_1, residual_1, chunk)
    update_users(item_next, residual_1, middle_user(user_t_last))

    far_copy.wait_recv()

    def back_copy(chunk):
        rows = pl.ds(chunk * wide, wide)
        return pltpu.make_async_remote_copy(
            src_ref=far_part.at[rows, :], dst_ref=friend_part.at[rows, :],
            send_sem=back_send.at[chunk], recv_sem=back_recv.at[chunk],
            device_id=(partner, g), device_id_type=MESH,
        )

    for chunk in range(friend_tiles // 2):
        prepared_residual(far_low, observed_2, residual_2, chunk)
        product = right_products(user_t_last, residual_2, chunk)
        far_part[pl.ds(chunk * wide, wide), :] = product.T.astype(bf16)
        back_copy(chunk).start()
        if chunk < chunks:
            send_parts(1, user_t, residual_1, chunk)

    def last_user(pair, rows, state, accum):
        user[rows, :] = state
        for k in range(2):
            user_accum[pl.ds(2 * pair + k, 1), :] = accum[k * edge : (k + 1) * edge].T[0:1, :]

    update_users(far_low, residual_2, last_user)
    stores = [
        pltpu.make_async_copy(user, user_out, store_sem.at[0]),
        pltpu.make_async_copy(user_accum, user_acc_out, store_sem.at[1]),
    ]
    for store in stores:
        store.start()

    ship_copy.wait_recv()
    share = shipped[pl.ds(0, edge), :]
    share_acc = as_columns(shipped[pl.ds(edge, 1), :], edge)
    share, share_acc = row_update(share, share_acc, shrinkage * share - part_total(1))
    share_end[...] = share
    share_acc_end[...] = share_acc.T[0:1, :]
    ends = [(share_end, item_out), (share_acc_end, item_acc_out)]
    for src, dst in ends:
        stores.append(pltpu.make_async_copy(src, dst, store_sem.at[len(stores)]))
        stores[-1].start()

    for chunk in range(friend_tiles // 2):
        back_copy(chunk).wait_recv()
        for k in range(2):
            tile = 2 * chunk + k
            rows = pl.ds(tile * edge, edge)
            state = friend[rows, :]
            gradient = shrinkage * state - friend_part[rows, :].astype(f32)
            state, accum = row_update(state, friend_acc[rows, :], gradient)
            friend[rows, :] = state
            friend_accum[pl.ds(tile, 1), :] = accum.T[0:1, :]
        rows = pl.ds(chunk * wide, wide)
        stores.append(
            pltpu.make_async_copy(
                friend.at[rows, :], friend_out.at[rows, :], store_sem.at[len(stores)]
            )
        )
        stores[-1].start()
    stores.append(
        pltpu.make_async_copy(friend_accum, friend_acc_out, store_sem.at[len(stores)])
    )
    stores[-1].start()

    for store in stores:
        store.wait()
    far_copy.wait_send()
    for stratum in range(2):
        for owner in range(groups):
            @pl.when(owner != g)
            def _():
                part_copy(stratum, owner, g).wait_send()
    for copy in low_copies:
        copy.wait_send()
    ship_copy.wait_send()
    for chunk in range(friend_tiles // 2):
        back_copy(chunk).wait_send()


def finish_kernel(count, *refs):
    sources, targets, held = refs[:count], refs[count : 2 * count], refs[2 * count : -2]
    fills = [
        pltpu.make_async_copy(sources[n], held[n], refs[-2].at[n]) for n in range(count)
    ]
    drains = [
        pltpu.make_async_copy(held[n], targets[n], refs[-1].at[n]) for n in range(count)
    ]
    for copy in fills:
        copy.start()
    for fill, drain in zip(fills, drains):
        fill.wait()
        drain.start()
    for copy in drains:
        copy.wait()


def local(
    user_factors, user_accum, friend_factors, friend_accum, item_factors, item_accum,
    rating_values, rating_masks, rating_rows, rating_cols, rating_counts,
    trust_values, trust_masks, trust_rows, trust_cols, trust_counts,
):
    blocks, groups = lax.axis_size("blk"), lax.axis_size("grp")
    edge, rank = rating_values.shape[-1], user_factors.shape[-1]
    users, items, friends = (
        user_factors.shape[0], item_factors.shape[0], friend_factors.shape[0]
    )
    user_tiles, item_tiles, friend_tiles = users // edge, items // edge, friends // edge
    assert edge == rank and items == groups * edge and blocks > 2
    assert user_tiles % 2 == 0 and item_tiles % 2 == 0 and friend_tiles % 2 == 0
    hbm = pl.BlockSpec(memory_space=pltpu.HBM)
    dma = pltpu.SemaphoreType.DMA
    flops = 6 * rank * users * (2 * items + friends)
    shapes = [
        jax.ShapeDtypeStruct((users, rank), f32),
        jax.ShapeDtypeStruct((user_tiles, edge), f32),
        jax.ShapeDtypeStruct((friends, rank), f32),
        jax.ShapeDtypeStruct((friend_tiles, edge), f32),
        jax.ShapeDtypeStruct((edge, rank), f32),
        jax.ShapeDtypeStruct((1, edge), f32),
    ]
    rate_slots, mask_words = rating_masks.shape[1:3]
    trust_slots = trust_masks.shape[0]
    results = pl.pallas_call(
        functools.partial(strata_kernel, blocks, groups),
        out_shape=shapes,
        in_specs=[hbm] * 16,
        out_specs=[hbm] * 6,
        scratch_shapes=[
            pltpu.VMEM((users, rank), f32),
            pltpu.VMEM((users, edge), f32),
            pltpu.VMEM((users, rank), bf16),
            pltpu.VMEM((rank, users), bf16),
            pltpu.VMEM((rank, users), bf16),
            pltpu.VMEM((friends, rank), f32),
            pltpu.VMEM((friends, rank), bf16),
            pltpu.VMEM((friends, rank), bf16),
            pltpu.VMEM((items, rank), f32),
            pltpu.VMEM((items, rank), bf16),
            pltpu.VMEM((items, rank), bf16),
            pltpu.VMEM(rating_values.shape[1:], bf16),
            pltpu.VMEM(rating_values.shape[1:], bf16),
            pltpu.VMEM(trust_values.shape, bf16),
            pltpu.VMEM((mask_words, rate_slots + 8, edge), jnp.int32),
            pltpu.VMEM((mask_words, rate_slots + 8, edge), jnp.int32),
            pltpu.VMEM((mask_words, trust_slots + 8, edge), jnp.int32),
            pltpu.VMEM((edge, edge), jnp.int32),
            pltpu.VMEM((users, items), bf16),
            pltpu.VMEM((users, items), bf16),
            pltpu.VMEM((users, friends), bf16),
            pltpu.VMEM((users, items), bf16),
            pltpu.VMEM((users, friends), bf16),
            pltpu.VMEM((friends, edge), f32),
            pltpu.VMEM((user_tiles, edge), f32),
            pltpu.VMEM((friend_tiles, edge), f32),
            pltpu.VMEM((item_tiles, edge), f32),
            pltpu.VMEM((2, rate_slots), jnp.int32),
            pltpu.VMEM((2, rate_slots), jnp.int32),
            pltpu.VMEM((1, 2), jnp.int32),
            pltpu.VMEM((1, trust_slots), jnp.int32),
            pltpu.VMEM((1, trust_slots), jnp.int32),
            pltpu.VMEM((1, 1), jnp.int32),
            pltpu.VMEM((8, edge), jnp.int32),
            pltpu.VMEM((8, edge), jnp.int32),
            pltpu.SMEM((8, edge), jnp.int32),
            pltpu.VMEM((groups, edge, rank), f32),
            pltpu.VMEM((groups, edge, rank), bf16),
            pltpu.VMEM((groups, edge, rank), f32),
            pltpu.VMEM((groups, edge, rank), bf16),
            pltpu.VMEM((edge, rank), f32),
            pltpu.VMEM((1, edge), f32),
            pltpu.VMEM((edge, rank), bf16),
            pltpu.VMEM((edge + 8, rank), f32),
            pltpu.VMEM((edge + 8, rank), f32),
            pltpu.VMEM((friends, rank), bf16),
            pltpu.VMEM((friends, rank), bf16),
            dma((18,)), dma((5 + friend_tiles // 2,)), dma,
            dma, dma,
            dma((2, groups)), dma((2, groups)),
            dma((groups,)), dma((groups,)),
            dma, dma,
            dma((friend_tiles // 2,)), dma((friend_tiles // 2,)),
        ],
        compiler_params=pltpu.CompilerParams(
            collective_id=0, has_side_effects=True, vmem_limit_bytes=58 * 1024 * 1024
        ),
        cost_estimate=pl.CostEstimate(
            flops=flops, bytes_accessed=8 * 1024 * 1024, transcendentals=0
        ),
        name="strata",
    )(
        user_factors, friend_factors, item_factors,
        user_accum.reshape(user_tiles, edge),
        friend_accum.reshape(friend_tiles, edge),
        item_accum.reshape(item_tiles, edge),
        rating_rows, rating_cols, rating_counts.T,
        trust_rows.reshape(1, -1), trust_cols.reshape(1, -1), trust_counts.reshape(1, 1),
        rating_values, rating_masks.transpose(0, 2, 1, 3),
        trust_values, trust_masks.transpose(1, 0, 2),
    )
    results = pl.pallas_call(
        functools.partial(finish_kernel, len(shapes)),
        out_shape=shapes,
        in_specs=[hbm] * len(shapes),
        out_specs=[hbm] * len(shapes),
        scratch_shapes=[pltpu.VMEM(shape.shape, shape.dtype) for shape in shapes]
        + [dma((len(shapes),)), dma((len(shapes),))],
        compiler_params=pltpu.CompilerParams(vmem_limit_bytes=58 * 1024 * 1024),
        name="finish",
    )(*results)
    return tuple(
        result.reshape(-1) if n % 2 else result for n, result in enumerate(results)
    )


def solution(mesh):
    split = P(("blk", "grp"))
    second = P(None, ("blk", "grp"))
    return jax.shard_map(
        local,
        mesh=mesh,
        in_specs=(
            split, split, split, split, P("blk"), P("blk"),
            second, second, second, second, second,
            split, split, split, split, split,
        ),
        out_specs=(split,) * 6,
        check_vma=False,
    )
```

```python
import functools

import jax
import jax.numpy as jnp
from jax import lax
from jax.experimental import pallas as pl
from jax.experimental.pallas import tpu as pltpu
from jax.sharding import PartitionSpec as P

learn_rate = 0.3
shrinkage = 0.02
word_bits = 14
MESH = pl.DeviceIdType.MESH
f32, bf16 = jnp.float32, jnp.bfloat16


def slot_table(seats, tables, edge):
    seats[...] = jnp.full_like(seats[...], -2 * edge)
    for n, (rows, cols, count, across, _) in enumerate(tables):
        place = rows * across + cols
        slot = lax.broadcasted_iota(jnp.int32, place.shape, 1)
        seats[n : n + 1, 0 : place.shape[1]] = jnp.where(slot < count, place, -2 * edge)
    lane = lax.broadcasted_iota(jnp.int32, (edge, edge), 1)
    sub = lax.broadcasted_iota(jnp.int32, (edge, edge), 0)
    line = jnp.zeros((1, edge), jnp.int32)
    base = 0
    for n, (rows, _, _, _, places) in enumerate(tables):
        hit = as_columns(seats[n : n + 1, :], edge) == lane - base
        found = jnp.sum(jnp.where(hit, sub + 1, 0), axis=0, keepdims=True)
        entry = jnp.where(found > 0, found - 1, rows.shape[1])
        inside = (lane[0:1] >= base) & (lane[0:1] < base + places)
        line = jnp.where(inside, entry, line)
        base += places
    assert base <= edge
    return line


def spread(words, edge):
    sub = lax.broadcasted_iota(jnp.int32, (8, words.shape[2]), 0)
    pieces = []
    for first in range(0, edge, 8):
        low, high = first // word_bits, (first + 7) // word_bits
        piece = jnp.broadcast_to(words[low], sub.shape)
        if high != low:
            after = jnp.broadcast_to(words[high], sub.shape)
            piece = jnp.where(sub < high * word_bits - first, piece, after)
        pieces.append(piece)
    return jnp.concatenate(pieces, axis=0)


def as_columns(row, edge):
    return jnp.broadcast_to(row, (edge, edge)).T


def row_update(factor, accum, gradient):
    new_accum = accum + jnp.mean(gradient * gradient, axis=-1, keepdims=True)
    return factor - learn_rate * gradient * lax.rsqrt(new_accum), new_accum


def strata_kernel(
    blocks, groups,
    user_hbm, friend_hbm, item_hbm, user_accum_hbm, friend_accum_hbm, item_accum_hbm,
    rate_rows_hbm, rate_cols_hbm, rate_counts_hbm,
    trust_rows_hbm, trust_cols_hbm, trust_counts_hbm,
    rate_values, rate_masks, trust_values, trust_masks,
    user_out, user_acc_out, friend_out, friend_acc_out, item_out, item_acc_out,
    user, user_acc, user_low, user_t, user_t_last, friend, friend_low, far_low, item, item_low, item_next,
    values_0, values_1, values_2, masks_0, masks_1, masks_2, bits,
    residual, residual_1, residual_2, observed_1, observed_2, friend_acc,
    user_accum, friend_accum, item_accum,
    rate_rows, rate_cols, rate_counts, trust_rows, trust_cols, trust_counts,
    seats, line, table, part_0, part_1, gathered_0, gathered_1, share_end, share_acc_end,
    share_low, ship, shipped, far_part, friend_part,
    load_sem, store_sem, table_sem, far_send, far_recv, part_send, part_recv, low_send, low_recv,
    ship_send, ship_recv, back_send, back_recv,
):
    b, g = lax.axis_index("blk"), lax.axis_index("grp")
    after = lax.rem(b + 1, blocks)
    before = lax.rem(b + blocks - 1, blocks)
    partner = lax.rem(b + blocks // 2, blocks)
    edge = bits.shape[0]
    wide = 2 * edge
    user_tiles, item_tiles, friend_tiles = (
        rows.shape[0] // edge for rows in (user, item, friend)
    )

    barrier = pltpu.get_barrier_semaphore()
    for step in range(1, groups):
        pl.semaphore_signal(
            barrier, inc=1, device_id=(b, lax.rem(g + step, groups)), device_id_type=MESH
        )
    for other in range(groups):
        pl.semaphore_signal(barrier, inc=1, device_id=(before, other), device_id_type=MESH)
    pl.semaphore_signal(barrier, inc=1, device_id=(partner, g), device_id_type=MESH)

    part, gathered = (part_0, part_1), (gathered_0, gathered_1)
    rate_slots, trust_slots = values_0.shape[0], values_2.shape[0]
    pairs = [
        (rate_rows_hbm, rate_rows), (rate_cols_hbm, rate_cols), (rate_counts_hbm, rate_counts),
        (trust_rows_hbm, trust_rows), (trust_cols_hbm, trust_cols),
        (trust_counts_hbm, trust_counts),
        (user_accum_hbm, user_accum), (friend_accum_hbm, friend_accum),
        (item_accum_hbm, item_accum),
        (user_hbm, user), (item_hbm, item),
        (rate_masks.at[0], masks_0.at[:, pl.ds(0, rate_slots), :]),
        (rate_values.at[0], values_0),
        (friend_hbm, friend),
        (rate_masks.at[1], masks_1.at[:, pl.ds(0, rate_slots), :]),
        (rate_values.at[1], values_1),
        (trust_masks, masks_2.at[:, pl.ds(0, trust_slots), :]),
        (trust_values, values_2),
    ]
    loads = [
        pltpu.make_async_copy(src, dst, load_sem.at[n]) for n, (src, dst) in enumerate(pairs)
    ]
    for load in loads[:13]:
        load.start()

    place = lax.broadcasted_iota(jnp.int32, bits.shape, 0)
    bits[...] = jnp.left_shift(jnp.ones_like(place), lax.rem(place, word_bits))

    for masks in (masks_0, masks_1, masks_2):
        spare = masks.shape[1] - 8
        masks[:, pl.ds(spare, 8), :] = jnp.zeros((masks.shape[0], 8, edge), jnp.int32)

    far_copy = pltpu.make_async_remote_copy(
        src_ref=friend_low, dst_ref=far_low, send_sem=far_send, recv_sem=far_recv,
        device_id=(partner, g), device_id_type=MESH,
    )

    for n in range(9):
        loads[n].wait()
    tables = [
        (
            rate_rows[s : s + 1, :], rate_cols[s : s + 1, :], rate_counts[:, s : s + 1],
            item_tiles, user_tiles * item_tiles,
        )
        for s in range(2)
    ]
    tables.append(
        (
            trust_rows[...], trust_cols[...], trust_counts[...],
            friend_tiles, user_tiles * friend_tiles,
        )
    )
    line[...] = jnp.broadcast_to(slot_table(seats, tables, edge), line.shape)
    table_copy = pltpu.make_async_copy(line, table, table_sem)
    table_copy.start()

    def tile_rows(tile):
        return pl.ds(pl.multiple_of(tile * edge, edge), edge)

    def keep_user(target_t, rows, state):
        user_low[rows, :] = state.astype(bf16)
        target_t[:, rows] = state.T.astype(bf16)

    loads[9].wait()
    loads[10].wait()
    for tile in range(user_tiles):
        rows = pl.ds(tile * edge, edge)
        keep_user(user_t, rows, user[rows, :])
    item_low[...] = item[...].astype(bf16)
    table_copy.wait()

    def tile_operands(values, masks, index):
        slot = table[0, index]
        seen = (spread(masks[:, pl.ds(slot, 1), :], edge) & bits[...]) != 0
        return seen, values[jnp.minimum(slot, values.shape[0] - 1)]

    def wide_columns(chunk):
        return pl.ds(pl.multiple_of(chunk * wide, wide), wide)

    def prepare(held, observed, values, masks, base, col_tiles):
        for r in range(user_tiles):
            for c in range(col_tiles):
                seen, value = tile_operands(values, masks, base + r * col_tiles + c)
                at = pl.ds(r * edge, edge), pl.ds(c * edge, edge)
                held[at] = jnp.where(seen, value.astype(f32), 0.0).astype(bf16)
                observed[at] = jnp.where(seen, 1.0, 0.0).astype(bf16)

    def predicted(right_low, pair, columns):
        return lax.dot_general(
            user_low[pl.ds(pair * wide, wide), :], right_low[columns, :],
            (((1,), (1,)), ((), ())), preferred_element_type=f32,
        )

    def direct_residual(right_low, values, masks, base, col_tiles, chunk):
        for pair in range(user_tiles // 2):
            predict = predicted(right_low, pair, wide_columns(chunk))
            for i in range(2):
                for k in range(2):
                    seen, value = tile_operands(
                        values, masks, base + (2 * pair + i) * col_tiles + 2 * chunk + k
                    )
                    error = value.astype(f32) - (
                        predict[i * edge : (i + 1) * edge, k * edge : (k + 1) * edge]
                    )
                    residual[
                        pl.ds((2 * pair + i) * edge, edge),
                        pl.ds(pl.multiple_of(chunk * wide + k * edge, edge), edge),
                    ] = jnp.where(seen, error, 0.0).astype(bf16)

    def prepared_residual(right_low, observed, held, chunk):
        columns = wide_columns(chunk)
        for pair in range(user_tiles // 2):
            rows = pl.ds(pair * wide, wide)
            predict = predicted(right_low, pair, columns)
            held[rows, columns] = (
                held[rows, columns].astype(f32) - observed[rows, columns].astype(f32) * predict
            ).astype(bf16)

    def right_products(left_t, held, chunk):
        return jnp.dot(
            left_t[...], held[:, wide_columns(chunk)], preferred_element_type=f32
        )

    def update_users(right_low, held, finish):
        for pair in range(user_tiles // 2):
            rows = pl.ds(pair * wide, wide)
            product = jnp.dot(
                held[rows, :], right_low[...], preferred_element_type=f32
            )
            state = user[rows, :]
            state, accum = row_update(state, user_acc[rows, :], shrinkage * state - product)
            finish(pair, rows, state, accum)

    def part_copy(stratum, owner, source):
        return pltpu.make_async_remote_copy(
            src_ref=part[stratum].at[owner], dst_ref=gathered[stratum].at[source],
            send_sem=part_send.at[stratum, owner], recv_sem=part_recv.at[stratum, source],
            device_id=(b, owner), device_id_type=MESH,
        )

    def send_parts(stratum, left_t, held, chunk):
        product = right_products(left_t, held, chunk)
        for k in range(2):
            owner = 2 * chunk + k
            piece = product[:, k * edge : (k + 1) * edge].T.astype(part[stratum].dtype)
            part[stratum][owner] = piece

            @pl.when(owner != g)
            def _():
                part_copy(stratum, owner, g).start()

            @pl.when(owner == g)
            def _():
                gathered[stratum][g] = piece

    def part_total(stratum):
        for source in range(groups):
            @pl.when(source != g)
            def _():
                part_copy(stratum, source, source).wait_recv()

        total = gathered[stratum][0].astype(f32)
        for source in range(1, groups):
            total = total + gathered[stratum][source].astype(f32)
        return total

    loads[11].wait()
    loads[12].wait()
    for load in loads[13:]:
        load.start()
    chunks = item_tiles // 2
    near = lax.div(g, 2)
    for step in range(chunks):
        chunk = lax.rem(near + 1 + step, chunks)
        direct_residual(item_low, values_0, masks_0, 0, item_tiles, chunk)
        if step == 0:
            pl.semaphore_wait(barrier, 2 * groups)
        send_parts(0, user_t, residual, chunk)

    for tile in range(user_tiles):
        user_acc[pl.ds(tile * edge, edge), :] = as_columns(user_accum[pl.ds(tile, 1), :], edge)
    loads[13].wait()
    friend_low[...] = friend[...].astype(bf16)
    far_copy.start()

    def middle_user(target_t):
        def finish(pair, rows, state, accum):
            user[rows, :] = state
            user_acc[rows, :] = accum
            keep_user(target_t, rows, state)

        return finish

    update_users(item_low, residual, middle_user(user_t))
    loads[14].wait()
    loads[15].wait()
    prepare(residual_1, observed_1, values_1, masks_1, user_tiles * item_tiles, item_tiles)

    share = item[tile_rows(g), :]
    share, share_acc = row_update(
        share, as_columns(item_accum[pl.ds(g, 1), :], edge), shrinkage * share - part_total(0)
    )
    share_low[...] = share.astype(bf16)
    low_copies = [
        pltpu.make_async_remote_copy(
            src_ref=share_low, dst_ref=item_next.at[tile_rows(g), :],
            send_sem=low_send.at[step], recv_sem=low_recv.at[g],
            device_id=(after, lax.rem(g + groups // 2 + step, groups)), device_id_type=MESH,
        )
        for step in range(groups)
    ]
    for copy in low_copies:
        copy.start()
    ship[pl.ds(0, edge), :] = share
    ship[pl.ds(edge, 8), :] = share_acc.T[0:8, :]
    ship_copy = pltpu.make_async_remote_copy(
        src_ref=ship, dst_ref=shipped, send_sem=ship_send, recv_sem=ship_recv,
        device_id=(after, g), device_id_type=MESH,
    )
    ship_copy.start()

    loads[16].wait()
    loads[17].wait()
    prepare(
        residual_2, observed_2, values_2, masks_2, 2 * user_tiles * item_tiles, friend_tiles
    )
    for tile in range(friend_tiles):
        friend_acc[pl.ds(tile * edge, edge), :] = as_columns(
            friend_accum[pl.ds(tile, 1), :], edge
        )
    for step in range(chunks):
        chunk = lax.rem(near + step, chunks)
        for k in range(2):
            source = 2 * chunk + k
            pltpu.make_async_remote_copy(
                src_ref=share_low, dst_ref=item_next.at[tile_rows(source), :],
                send_sem=low_send.at[source], recv_sem=low_recv.at[source],
                device_id=(after, source), device_id_type=MESH,
            ).wait_recv()
        prepared_residual(item_next, observed_1, residual_1, chunk)
    update_users(item_next, residual_1, middle_user(user_t_last))

    far_copy.wait_recv()

    def back_copy(chunk):
        rows = pl.ds(chunk * wide, wide)
        return pltpu.make_async_remote_copy(
            src_ref=far_part.at[rows, :], dst_ref=friend_part.at[rows, :],
            send_sem=back_send.at[chunk], recv_sem=back_recv.at[chunk],
            device_id=(partner, g), device_id_type=MESH,
        )

    for chunk in range(friend_tiles // 2):
        prepared_residual(far_low, observed_2, residual_2, chunk)
        product = right_products(user_t_last, residual_2, chunk)
        far_part[pl.ds(chunk * wide, wide), :] = product.T.astype(bf16)
        back_copy(chunk).start()
        if chunk < chunks:
            send_parts(1, user_t, residual_1, chunk)

    def last_user(pair, rows, state, accum):
        user[rows, :] = state
        for k in range(2):
            user_accum[pl.ds(2 * pair + k, 1), :] = accum[k * edge : (k + 1) * edge].T[0:1, :]

    update_users(far_low, residual_2, last_user)
    stores = [
        pltpu.make_async_copy(user, user_out, store_sem.at[0]),
        pltpu.make_async_copy(user_accum, user_acc_out, store_sem.at[1]),
    ]
    for store in stores:
        store.start()

    ship_copy.wait_recv()
    share = shipped[pl.ds(0, edge), :]
    share_acc = as_columns(shipped[pl.ds(edge, 1), :], edge)
    share, share_acc = row_update(share, share_acc, shrinkage * share - part_total(1))
    share_end[...] = share
    share_acc_end[...] = share_acc.T[0:1, :]
    ends = [(share_end, item_out), (share_acc_end, item_acc_out)]
    for src, dst in ends:
        stores.append(pltpu.make_async_copy(src, dst, store_sem.at[len(stores)]))
        stores[-1].start()

    for chunk in range(friend_tiles // 2):
        back_copy(chunk).wait_recv()
        for k in range(2):
            tile = 2 * chunk + k
            rows = pl.ds(tile * edge, edge)
            state = friend[rows, :]
            gradient = shrinkage * state - friend_part[rows, :].astype(f32)
            state, accum = row_update(state, friend_acc[rows, :], gradient)
            friend[rows, :] = state
            friend_accum[pl.ds(tile, 1), :] = accum.T[0:1, :]
        rows = pl.ds(chunk * wide, wide)
        stores.append(
            pltpu.make_async_copy(
                friend.at[rows, :], friend_out.at[rows, :], store_sem.at[len(stores)]
            )
        )
        stores[-1].start()
    stores.append(
        pltpu.make_async_copy(friend_accum, friend_acc_out, store_sem.at[len(stores)])
    )
    stores[-1].start()

    for store in stores:
        store.wait()
    far_copy.wait_send()
    for stratum in range(2):
        for owner in range(groups):
            @pl.when(owner != g)
            def _():
                part_copy(stratum, owner, g).wait_send()
    for copy in low_copies:
        copy.wait_send()
    ship_copy.wait_send()
    for chunk in range(friend_tiles // 2):
        back_copy(chunk).wait_send()


def result_pieces(shapes):
    return [
        (n, first, min(256, shape.shape[0] - first))
        for n, shape in enumerate(shapes)
        for first in range(0, shape.shape[0], 256)
    ]


def finish_kernel(pieces, count, *refs):
    sources, targets, held = refs[:count], refs[count : 2 * count], refs[2 * count : -2]

    def copies(froms, tos, sems):
        return [
            pltpu.make_async_copy(
                froms[n].at[pl.ds(first, rows), :], tos[n].at[pl.ds(first, rows), :], sems.at[m]
            )
            for m, (n, first, rows) in enumerate(pieces)
        ]

    fills = copies(sources, held, refs[-2])
    drains = copies(held, targets, refs[-1])
    for copy in fills:
        copy.start()
    for fill, drain in zip(fills, drains):
        fill.wait()
        drain.start()
    for copy in drains:
        copy.wait()


def local(
    user_factors, user_accum, friend_factors, friend_accum, item_factors, item_accum,
    rating_values, rating_masks, rating_rows, rating_cols, rating_counts,
    trust_values, trust_masks, trust_rows, trust_cols, trust_counts,
):
    blocks, groups = lax.axis_size("blk"), lax.axis_size("grp")
    edge, rank = rating_values.shape[-1], user_factors.shape[-1]
    users, items, friends = (
        user_factors.shape[0], item_factors.shape[0], friend_factors.shape[0]
    )
    user_tiles, item_tiles, friend_tiles = users // edge, items // edge, friends // edge
    assert edge == rank and items == groups * edge and blocks > 2
    assert user_tiles % 2 == 0 and item_tiles % 2 == 0 and friend_tiles % 2 == 0
    hbm = pl.BlockSpec(memory_space=pltpu.HBM)
    dma = pltpu.SemaphoreType.DMA
    flops = 6 * rank * users * (2 * items + friends)
    shapes = [
        jax.ShapeDtypeStruct((users, rank), f32),
        jax.ShapeDtypeStruct((user_tiles, edge), f32),
        jax.ShapeDtypeStruct((friends, rank), f32),
        jax.ShapeDtypeStruct((friend_tiles, edge), f32),
        jax.ShapeDtypeStruct((edge, rank), f32),
        jax.ShapeDtypeStruct((1, edge), f32),
    ]
    pieces = result_pieces(shapes)
    rate_slots, mask_words = rating_masks.shape[1:3]
    trust_slots = trust_masks.shape[0]
    results = pl.pallas_call(
        functools.partial(strata_kernel, blocks, groups),
        out_shape=shapes,
        in_specs=[hbm] * 16,
        out_specs=[hbm] * 6,
        scratch_shapes=[
            pltpu.VMEM((users, rank), f32),
            pltpu.VMEM((users, edge), f32),
            pltpu.VMEM((users, rank), bf16),
            pltpu.VMEM((rank, users), bf16),
            pltpu.VMEM((rank, users), bf16),
            pltpu.VMEM((friends, rank), f32),
            pltpu.VMEM((friends, rank), bf16),
            pltpu.VMEM((friends, rank), bf16),
            pltpu.VMEM((items, rank), f32),
            pltpu.VMEM((items, rank), bf16),
            pltpu.VMEM((items, rank), bf16),
            pltpu.VMEM(rating_values.shape[1:], bf16),
            pltpu.VMEM(rating_values.shape[1:], bf16),
            pltpu.VMEM(trust_values.shape, bf16),
            pltpu.VMEM((mask_words, rate_slots + 8, edge), jnp.int32),
            pltpu.VMEM((mask_words, rate_slots + 8, edge), jnp.int32),
            pltpu.VMEM((mask_words, trust_slots + 8, edge), jnp.int32),
            pltpu.VMEM((edge, edge), jnp.int32),
            pltpu.VMEM((users, items), bf16),
            pltpu.VMEM((users, items), bf16),
            pltpu.VMEM((users, friends), bf16),
            pltpu.VMEM((users, items), bf16),
            pltpu.VMEM((users, friends), bf16),
            pltpu.VMEM((friends, edge), f32),
            pltpu.VMEM((user_tiles, edge), f32),
            pltpu.VMEM((friend_tiles, edge), f32),
            pltpu.VMEM((item_tiles, edge), f32),
            pltpu.VMEM((2, rate_slots), jnp.int32),
            pltpu.VMEM((2, rate_slots), jnp.int32),
            pltpu.VMEM((1, 2), jnp.int32),
            pltpu.VMEM((1, trust_slots), jnp.int32),
            pltpu.VMEM((1, trust_slots), jnp.int32),
            pltpu.VMEM((1, 1), jnp.int32),
            pltpu.VMEM((8, edge), jnp.int32),
            pltpu.VMEM((8, edge), jnp.int32),
            pltpu.SMEM((8, edge), jnp.int32),
            pltpu.VMEM((groups, edge, rank), f32),
            pltpu.VMEM((groups, edge, rank), bf16),
            pltpu.VMEM((groups, edge, rank), f32),
            pltpu.VMEM((groups, edge, rank), bf16),
            pltpu.VMEM((edge, rank), f32),
            pltpu.VMEM((1, edge), f32),
            pltpu.VMEM((edge, rank), bf16),
            pltpu.VMEM((edge + 8, rank), f32),
            pltpu.VMEM((edge + 8, rank), f32),
            pltpu.VMEM((friends, rank), bf16),
            pltpu.VMEM((friends, rank), bf16),
            dma((18,)), dma((5 + friend_tiles // 2,)), dma,
            dma, dma,
            dma((2, groups)), dma((2, groups)),
            dma((groups,)), dma((groups,)),
            dma, dma,
            dma((friend_tiles // 2,)), dma((friend_tiles // 2,)),
        ],
        compiler_params=pltpu.CompilerParams(
            collective_id=0, has_side_effects=True, vmem_limit_bytes=58 * 1024 * 1024
        ),
        cost_estimate=pl.CostEstimate(
            flops=flops, bytes_accessed=8 * 1024 * 1024, transcendentals=0
        ),
        name="strata",
    )(
        user_factors, friend_factors, item_factors,
        user_accum.reshape(user_tiles, edge),
        friend_accum.reshape(friend_tiles, edge),
        item_accum.reshape(item_tiles, edge),
        rating_rows, rating_cols, rating_counts.T,
        trust_rows.reshape(1, -1), trust_cols.reshape(1, -1), trust_counts.reshape(1, 1),
        rating_values, rating_masks.transpose(0, 2, 1, 3),
        trust_values, trust_masks.transpose(1, 0, 2),
    )
    results = pl.pallas_call(
        functools.partial(finish_kernel, pieces, len(shapes)),
        out_shape=shapes,
        in_specs=[hbm] * len(shapes),
        out_specs=[hbm] * len(shapes),
        scratch_shapes=[pltpu.VMEM(shape.shape, shape.dtype) for shape in shapes]
        + [dma((len(pieces),)), dma((len(pieces),))],
        compiler_params=pltpu.CompilerParams(vmem_limit_bytes=58 * 1024 * 1024),
        name="finish",
    )(*results)
    return tuple(
        result.reshape(-1) if n % 2 else result for n, result in enumerate(results)
    )


def solution(mesh):
    split = P(("blk", "grp"))
    second = P(None, ("blk", "grp"))
    return jax.shard_map(
        local,
        mesh=mesh,
        in_specs=(
            split, split, split, split, P("blk"), P("blk"),
            second, second, second, second, second,
            split, split, split, split, split,
        ),
        out_specs=(split,) * 6,
        check_vma=False,
    )
```
